512 devices in a mesh: dp: 64 (over x, z), tensor: 8 (over y, core).
Axes of the slice: x: 4, y: 4, z: 16, core: 2. Of those that a mesh axis runs over, the one named last changes fastest.
Arguments:
- query_states: bfloat16 [256, 64, 4096], P('dp', None, 'tensor'), may hold values from -300 to 300
- passage_states: bfloat16 [256, 64, 4096], P('dp', None, 'tensor'), may hold values from -300 to 300
- negative_states: bfloat16 [256, 64, 4096], P('dp', None, 'tensor'), may hold values from -300 to 300
- query_len: int32 [256], P('dp'), may hold values from 4 to 64
- passage_len: int32 [256], P('dp'), may hold values from 4 to 64
- negative_len: int32 [256], P('dp'), may hold values from 4 to 64
- norm_gain: float32 [4096], P('tensor'), may hold values from 0.5 to 1.5
- proj_weight: bfloat16 [4096, 768], P('tensor'), may hold values from -0.09375 to 0.09375
- neg_owner: int32 [256, 7], P('dp'), may hold values from 0 to 63, all different within a row; in each aligned block of 4 rows (0 to 3, 4 to 7, ...) at most 4 rows name the same one
- neg_slot: int32 [256, 7], P('dp'), may hold values from 0 to 3
Outputs:
- grad_queries: bfloat16 [256, 64, 4096], P('dp', None, 'tensor')
- grad_passages: bfloat16 [256, 64, 4096], P('dp', None, 'tensor')
- grad_negatives: bfloat16 [256, 64, 4096], P('dp', None, 'tensor')
- grad_weight: bfloat16 [4096, 768], P('tensor')
- grad_gain: float32 [4096], P('tensor')
- loss: float32 [], replicated
The draws below stay inside these ranges and needn't reach their ends.
Inputs may be any that keep to these rules, and one draw needn't show every extreme that they name: `neg_owner`: each query names 7 different owners; among the 4 queries of one dp index no owner is named more than 4 times, and one owner exactly 4 times.
All inputs are finite; a program needn't handle non-finite values.
Results may differ from the reference program's by a relative error of at most 0.0017.
Values sent between devices are 32-bit elements; how exact they have to be, the bound alone decides.
A program may use at most 64 MiB of HBM per device.

```python
import math
import jax
import jax.numpy as jnp
import numpy as np
from jax import lax

D = 4096
E = 768
LEN = 64
NEGS = 7
CAP = 4
PAIRS_DEV = 4
PAIRS_ALL = 256
N_DP = 64


def layer_states(key, base):
    k_row, k_col = jax.random.split(key, 2)
    count = base.shape[0]
    rows = jnp.exp(jax.random.uniform(k_row, (count, LEN, 1), jnp.float32, 0.0, math.log(10.0)))
    cols = jnp.exp(jax.random.uniform(k_col, (1, 1, D), jnp.float32, 0.0, math.log(10.0)))
    values = base * rows * cols
    return jnp.clip(values, -300.0, 300.0).astype(jnp.bfloat16)


def base_draw(key):
    k_base, k_rest = jax.random.split(key)
    base = jax.random.normal(k_base, (PAIRS_ALL, LEN, D), jnp.float32)
    return layer_states(k_rest, base)


def draw_query_states(key, part):
    key = jax.random.fold_in(key, 11)
    return base_draw(key)


def draw_passage_states(key, part):
    key = jax.random.fold_in(key, 12)
    return base_draw(key)


def draw_negative_states(key, part):
    key = jax.random.fold_in(key, 13)
    return base_draw(key)


def set_ends(drawn, rng, smallest, top_value):
    spot = [jax.random.randint(jax.random.fold_in(rng, axis), (), 0, length) for axis, length in enumerate(drawn.shape)]
    main_axis = drawn.shape.index(max(drawn.shape))
    beside = spot[:main_axis] + [(spot[main_axis] + 1) % drawn.shape[main_axis]] + spot[main_axis + 1:]
    return drawn.at[tuple(spot)].set(smallest).at[tuple(beside)].set(top_value)


def level_of(stream_key, dims, shards, low, largest):
    factor_of = 1.0
    for axis_at, blocks in shards:
        steps = jax.random.uniform(jax.random.fold_in(jax.random.fold_in(stream_key, 6), axis_at), (blocks,), jnp.float32, low / len(shards), largest / len(shards))
        factor_of = factor_of * jnp.repeat(jnp.exp(steps), dims[axis_at] // blocks).reshape((-1,) + (1,) * (len(dims) - 1 - axis_at))
    return factor_of


def routed_block(key, own, number, rows, count, top, reach, lean):
    sequence = jax.random.permutation(key, count)
    packed, usual = shares(count, rows * top, reach, lean, True), shares(count, rows * top, reach, lean, False)
    places = jnp.arange(count)

    def named(sizes, rotation):
        used = int((sizes > 0).sum())
        fixed = max(1, used // 4)
        passed = fixed + (places - fixed + rotation * (used - fixed)) % max(1, count - fixed)
        return jnp.zeros((count,), jnp.int32).at[sequence[jnp.where(places < fixed, places, passed)]].set(jnp.asarray(sizes, jnp.int32))

    sizes = jnp.where(number % 4 == 0, named(packed, number // 4), named(usual, number - number // 4 - 1))
    mixed = jax.random.permutation(jax.random.fold_in(own, 3), count)
    source_of, taker = mixed[0:count // 2 * 2:2], mixed[1:count // 2 * 2:2]
    room = jnp.minimum(sizes[source_of] - 1, reach - sizes[taker]) // 2
    room = jnp.where((source_of == sequence[0]) | (taker == sequence[0]) | (sizes[taker] == 0), 0, jnp.maximum(room, 0))
    passed = jax.random.randint(jax.random.fold_in(own, 4), (count // 2,), 0, 1 << 20) % (room + 1)
    sizes = sizes.at[source_of].add(-passed).at[taker].add(passed)
    items = jnp.searchsorted(jnp.cumsum(sizes), jnp.arange(rows * top), side="right").astype(jnp.int32)
    table = items.reshape(top, rows).T
    table = table[jax.random.permutation(jax.random.fold_in(own, 1), rows)]
    rotation = jax.random.randint(jax.random.fold_in(own, 2), (rows, 1), 0, top)
    return jnp.take_along_axis(table, (jnp.arange(top)[None, :] + rotation) % top, axis=1)


def shares(amount, total, reach, slope, full):
    weights = [(1 << 20) // math.isqrt(grade ** slope) + 1 for grade in range(1, amount + 1)]
    largest = reach if full else min(reach, max(-(-total // amount), total * weights[0] // sum(weights)))
    least = 1 if total - largest >= amount - 1 else 0
    holding, spare = [largest] + [least] * (amount - 1), total - largest - least * (amount - 1)
    while spare > 0:
        movable = [i for i in range(1, amount) if holding[i] < largest] or [i for i in range(1, amount) if holding[i] < reach]
        pool, remaining = sum([weights[i] for i in movable]), spare
        for i in movable:
            extra = min(reach - holding[i], max(1, remaining * weights[i] // pool), spare)
            holding[i] = holding[i] + extra
            spare = spare - extra
    return np.array(holding)


def normal_values(stream_key, dims, spread, bound, cuts=(), dtype=jnp.bfloat16):
    factor_of = level_of(stream_key, dims, cuts, -0.22, 0.18) if cuts else 1.0
    array = jax.random.normal(stream_key, dims, jnp.float32) * spread * factor_of
    return jnp.minimum(jnp.maximum(array, -bound), bound).astype(dtype)


def setup_inputs(seed: int = 0) -> dict:
    key_list = jax.random.split(jax.random.key(seed), 11)
    query_states = draw_query_states(jax.random.fold_in(key_list[10], 71), 0)
    passage_states = draw_passage_states(jax.random.fold_in(key_list[10], 71), 0)
    negative_states = draw_negative_states(jax.random.fold_in(key_list[10], 71), 0)
    query_len = set_ends(jax.random.randint(key_list[3], (PAIRS_ALL,), 4, LEN + 1), jax.random.fold_in(key_list[3], 1), 4, LEN).astype(jnp.int32)
    passage_len = set_ends(jax.random.randint(key_list[4], (PAIRS_ALL,), 4, LEN + 1), jax.random.fold_in(key_list[4], 1), 4, LEN).astype(jnp.int32)
    negative_len = set_ends(jax.random.randint(key_list[5], (PAIRS_ALL,), 4, LEN + 1), jax.random.fold_in(key_list[5], 1), 4, LEN).astype(jnp.int32)
    norm_gain = jnp.clip(1.0 + 0.1 * jax.random.normal(key_list[6], (D,), jnp.float32), 0.5, 1.5)
    proj_weight = normal_values(key_list[7], (D, E), D ** -0.5, 0.09375, ((0, 8),))
    neg_owner_keys = jax.random.split(jax.random.fold_in(key_list[8], 1), PAIRS_ALL // PAIRS_DEV)
    neg_owner_turns = jax.random.permutation(jax.random.fold_in(key_list[8], 3), PAIRS_ALL // PAIRS_DEV)
    neg_owner = jax.vmap(lambda own, number: routed_block(jax.random.fold_in(key_list[8], 2), own, number, PAIRS_DEV, N_DP, NEGS, CAP, 2))(neg_owner_keys, neg_owner_turns).reshape((PAIRS_ALL, NEGS))
    neg_slot = set_ends(jax.random.randint(key_list[9], (PAIRS_ALL, NEGS), 0, PAIRS_DEV), jax.random.fold_in(key_list[9], 1), 0, PAIRS_DEV - 1).astype(jnp.int32)
    return {"query_states": query_states, "passage_states": passage_states, "negative_states": negative_states, "query_len": query_len, "passage_len": passage_len, "negative_len": negative_len, "norm_gain": norm_gain, "proj_weight": proj_weight, "neg_owner": neg_owner, "neg_slot": neg_slot}


score_scale = 20.0
loss_scale = 1024.0
epsilon = 1e-06

def encode(states, lengths, gain, weight):
    squares = lax.optimization_barrier(jnp.sum(states * states, -1, keepdims=True))
    scales = lax.rsqrt(squares / D + epsilon)
    live = (jnp.arange(LEN)[None, :] < lengths[:, None]).astype(jnp.float32) / lengths[:, None].astype(jnp.float32)
    pooled = lax.optimization_barrier(jnp.sum(states * scales * live[:, :, None], 1)) * gain
    proj = jnp.dot(pooled, weight, precision=lax.Precision.HIGHEST)
    return proj / jnp.sqrt(lax.optimization_barrier(jnp.sum(proj * proj, -1, keepdims=True)) + epsilon)

def forward_units(states, lengths, gain, weight):
    shaped = states.reshape(N_DP, PAIRS_DEV, LEN, D)
    sizes = lengths.reshape(N_DP, PAIRS_DEV)

    def single(items):
        return encode(items[0].astype(jnp.float32), items[1], gain, weight)
    return lax.map(single, (shaped, sizes)).reshape(PAIRS_ALL, E)

def backward_units(states, lengths, cotangent, gain, weight):
    shaped = states.reshape(N_DP, PAIRS_DEV, LEN, D)
    sizes = lengths.reshape(N_DP, PAIRS_DEV)
    cots = cotangent.reshape(N_DP, PAIRS_DEV, E)

    def single(items):
        block, size, cot = items

        def local(s, g, w):
            return encode(s, size, g, w)
        unit, back = jax.vjp(local, block.astype(jnp.float32), gain, weight)
        d_states, d_gain, d_weight = back(cot)
        return (d_states.astype(jnp.bfloat16), d_gain, d_weight)
    d_states, d_gain, d_weight = lax.map(single, (shaped, sizes, cots))
    return (d_states.reshape(PAIRS_ALL, LEN, D), lax.optimization_barrier(jnp.sum(d_gain, 0)), lax.optimization_barrier(jnp.sum(d_weight, 0)))

def objective(uq, up, un, ids):
    s_in = score_scale * jnp.dot(uq, up.T, precision=lax.Precision.HIGHEST)
    negs = un[ids]
    s_neg = score_scale * lax.optimization_barrier(jnp.sum(uq[:, None, :] * negs, -1))
    total = lax.optimization_barrier(jnp.sum(jnp.exp(s_in), 1)) + lax.optimization_barrier(jnp.sum(jnp.exp(s_neg), 1))
    return jnp.sum(jnp.log(total) - jnp.diagonal(s_in))

def reference(query_states, passage_states, negative_states, query_len, passage_len, negative_len, norm_gain, proj_weight, neg_owner, neg_slot):
    weight = proj_weight.astype(jnp.float32)
    uq = forward_units(query_states, query_len, norm_gain, weight)
    up = forward_units(passage_states, passage_len, norm_gain, weight)
    un = forward_units(negative_states, negative_len, norm_gain, weight)
    ids = (neg_owner * PAIRS_DEV + neg_slot).astype(jnp.int32)

    def scored(a, b, c):
        return objective(a, b, c, ids)
    value, back = jax.vjp(scored, uq, up, un)
    d_uq, d_up, d_un = back(jnp.ones_like(value) * loss_scale)
    g_q, gain_q, weight_q = backward_units(query_states, query_len, d_uq, norm_gain, weight)
    g_p, gain_p, weight_p = backward_units(passage_states, passage_len, d_up, norm_gain, weight)
    g_n, gain_n, weight_n = backward_units(negative_states, negative_len, d_un, norm_gain, weight)
    grad_weight = ((weight_q + weight_p + weight_n) / loss_scale).astype(jnp.bfloat16)
    grad_gain = (gain_q + gain_p + gain_n) / loss_scale
    return (g_q, g_p, g_n, grad_weight, grad_gain, value / PAIRS_ALL)
```

```python
import jax
import jax.numpy as jnp
from jax import lax
from jax.experimental import pallas as pl
from jax.experimental.pallas import tpu as pltpu
from jax.sharding import PartitionSpec as P

NX, NY, NZ, NC = 4, 4, 16, 2
NT = NY * NC
DP = NX * NZ
D = 4096
F = D // NT
E = 768
H = E // NC
LEN = 64
SLOTS = 4
NEGS = 7
KINDS = 3
TOK = KINDS * SLOTS * LEN
ALL = SLOTS * DP
SEQ = KINDS * ALL
score_scale = 20.0
loss_scale = 1024.0
epsilon = 1e-06
MESH = pl.DeviceIdType.MESH
f32 = jnp.float32
bf16 = jnp.bfloat16
NN = (((1,), (0,)), ((), ()))
NTD = (((1,), (1,)), ((), ()))


def dot(a, b, dims=NN):
    return lax.dot_general(a, b, dims, preferred_element_type=f32)


def exact_dot(a, b, dims=NN):
    return lax.dot_general(a, b, dims, preferred_element_type=f32, precision=lax.Precision.HIGHEST)


def split2(v):
    hi = v.astype(bf16)
    return hi, (v - hi.astype(f32)).astype(bf16)


def split3(v):
    hi = v.astype(bf16)
    rest = v - hi.astype(f32)
    mid = rest.astype(bf16)
    return jnp.concatenate([hi, mid, (rest - mid.astype(f32)).astype(bf16)], 0)


def join3(v):
    return v[0:16] + v[16:32] + v[32:48]


def dot3(a, b, dims=NN):
    return dot(a[0], b[0], dims) + (dot(a[0], b[1], dims) + dot(a[1], b[0], dims))


def kernel(
    x_refs,
    len_refs,
    gain_ref,
    w_ref,
    owner_ref,
    slot_ref,
    g_refs,
    gw_ref,
    gg_ref,
    loss_ref,
    xs,
    sq_own,
    sq_land,
    dot_own,
    dot_land,
    stage,
    rs_land,
    ids_ref,
    L,
    PB,
    u_hi,
    u_lo,
    dproj,
    own_rows,
    s_sq,
    r_sq,
    s_rs,
    r_rs,
    s_z,
    r_z,
    s_a,
    r_a,
    s_b,
    r_b,
    s_c,
    r_c,
    s_dot,
    r_dot,
    s_px,
    r_px,
    s_pz,
    r_pz,
):
    dp = lax.axis_index("dp")
    t = lax.axis_index("tensor")
    x, z = dp // NZ, dp % NZ
    y, c = t // NC, t % NC
    a = jnp.where(c == 0, x, y)
    b = jnp.where(c == 0, y, x)

    def tensor_peer(k):
        return (dp, (t + k) % NT)

    def x_peer(k):
        return (((x + k) % NX) * NZ + z, t)

    def y_peer(k):
        return (dp, ((y + k) % NY) * NC + c)

    def z_peer(k):
        return (x * NZ + (z + k) % NZ, t)

    def either(cond, p, q):
        return tuple(jnp.where(cond, i, j) for i, j in zip(p, q))

    def a_peer(k):
        return either(c == 0, x_peer(k), y_peer(k))

    def b_peer(k):
        return either(c == 0, y_peer(k), x_peer(k))

    sibling = (dp, y * NC + 1 - c)

    def send(src, dst, ss, rs, to):
        cp = pltpu.make_async_remote_copy(
            src_ref=src, dst_ref=dst, send_sem=ss, recv_sem=rs, device_id=to, device_id_type=MESH
        )
        cp.start()
        return cp

    barrier = pltpu.get_barrier_semaphore()
    greeted = (
        [tensor_peer(k) for k in range(1, NT)]
        + [x_peer(k) for k in range(1, NX)]
        + [z_peer(k) for k in range(1, NZ)]
    )
    for peer in greeted:
        pl.semaphore_signal(barrier, inc=1, device_id=peer, device_id_type=MESH)

    for i in range(KINDS):
        xs[pl.ds(i * SLOTS * LEN, SLOTS * LEN), :] = x_refs[i][...]
    xf = xs[...].astype(f32)
    xf = xf * xf
    part = (xf[:, 0:128] + xf[:, 128:256]) + (xf[:, 256:384] + xf[:, 384:512])
    sq_own[...] = exact_dot(jnp.ones((8, 128), f32), part, NTD)[0:1]

    pl.semaphore_wait(barrier, len(greeted))

    def tensor_sum(own, land, ss, rs):
        cps = [send(own, land.at[t], ss.at[k - 1], rs.at[k - 1], tensor_peer(k)) for k in range(1, NT)]
        land[t] = own[...]
        for cp in cps:
            cp.wait()
        total = land[0]
        for i in range(1, NT):
            total = total + land[i]
        return total

    squares = tensor_sum(sq_own, sq_land, s_sq, r_sq)
    scales = lax.rsqrt(squares / D + epsilon)
    lane = lax.broadcasted_iota(jnp.int32, (1, TOK), 1)
    seq = lane // LEN
    lens = jnp.zeros((1, TOK), jnp.int32)
    for i in range(KINDS):
        for s in range(SLOTS):
            lens = jnp.where(seq == i * SLOTS + s, len_refs[i][s], lens)
    live = jnp.where(lane % LEN < lens, 1.0 / lens.astype(f32), 0.0)
    coeffs = scales * live
    row = lax.broadcasted_iota(jnp.int32, (16, TOK), 0)
    mine = (row % 4) * SLOTS + row // 4 == seq
    plain = join3(dot(split3(jnp.where(mine, coeffs, 0.0)), xs[...]))
    PB[x, z] = plain
    px = [
        send(PB.at[x, z], PB.at[x, z], s_px.at[k - 1], r_px.at[k - 1], x_peer(k))
        for k in range(1, NX)
    ]
    gain = gain_ref[...]
    proj = join3(dot(split3(plain * gain), w_ref[...]))
    for s in range(SLOTS):
        for h in range(NC):
            stage[s * NC + h] = proj[4 * s : 4 * s + 4, h * H : (h + 1) * H]
    cps = [
        send(stage.at[(t + k) % NT], rs_land.at[t], s_rs.at[k - 1], r_rs.at[k - 1], tensor_peer(k))
        for k in range(1, NT)
    ]
    rs_land[t] = stage[t]
    ids = (slot_ref[...] * DP + owner_ref[...]).astype(f32)
    ids_ref[...] = jnp.zeros_like(ids_ref)
    for s in range(SLOTS):
        ids_ref[s, :, 0:NEGS] = ids[s : s + 1]
    for cp in cps:
        cp.wait()
    piece = rs_land[0]
    for i in range(1, NT):
        piece = piece + rs_land[i]
    place = lax.broadcasted_iota(jnp.int32, (4, H), 0)
    at = (b * 4 + a) * NZ + z
    L[c, at] = jnp.where(place == 3, ids_ref[y], piece)

    zs = [send(L.at[c, at], L.at[c, at], s_z.at[k - 1], r_z.at[k - 1], z_peer(k)) for k in range(1, NZ)]

    for cp in px:
        cp.wait()

    def ring(step):
        out = []
        if step <= 8:
            up = PB.at[:, (z - step + 1 + NZ) % NZ]
            out.append(send(up, up, s_pz.at[0, step - 1], r_pz.at[0, step - 1], z_peer(1)))
        if step <= 7:
            down = PB.at[:, (z + step - 1) % NZ]
            out.append(send(down, down, s_pz.at[1, step - 1], r_pz.at[1, step - 1], z_peer(NZ - 1)))
        return out

    turn = ring(1)

    def next_turn(turn, step):
        for cp in turn:
            cp.wait()
        return ring(step)

    for cp in zs:
        cp.wait()
    line = L.at[c, pl.ds((b * 4 + a) * NZ, NZ)]
    cps = [send(line, line, s_a.at[k - 1], r_a.at[k - 1], a_peer(k)) for k in range(1, 4)]
    turn = next_turn(turn, 2)
    for cp in cps:
        cp.wait()
    plane = L.at[c, pl.ds(b * 64, 64)]
    cps = [send(plane, plane, s_b.at[k - 1], r_b.at[k - 1], b_peer(k)) for k in range(1, 4)]
    across = [send(plane, plane, s_c.at[0], r_c.at[0], sibling)]
    turn = next_turn(turn, 3)
    for k in (1, 3, 2):
        cps[k - 1].wait()
        got = L.at[c, pl.ds(((b + 4 - k) % 4) * 64, 64)]
        across.append(send(got, got, s_c.at[k], r_c.at[k], sibling))
        turn = next_turn(turn, {1: 4, 3: 5, 2: 6}[k])
    for cp in across:
        cp.wait()

    for k in range(KINDS):
        for s in range(SLOTS):
            left = L[0, pl.ds(s * 64, 64), k, :]
            right = jnp.concatenate(
                [L[1, pl.ds(i * 64 + s * NZ, NZ), k, :] for i in range(NX)], 0
            )
            dproj[pl.ds(k * ALL + s * DP, DP), pl.ds(0, H)] = left
            dproj[pl.ds(k * ALL + s * DP, DP), pl.ds(H, H)] = right
    projs = dproj[...]
    r_norm = lax.rsqrt(jnp.sum(projs * projs, -1, keepdims=True) + epsilon)
    unit = projs * r_norm
    hi, lo = split2(unit)
    u_hi[...] = hi
    u_lo[...] = lo
    turn = next_turn(turn, 7)

    def part_of(k):
        rows = pl.ds(k * ALL, ALL)
        return u_hi[rows, :], u_lo[rows, :]

    uq, up, un = part_of(0), part_of(1), part_of(2)
    s_in = score_scale * dot3(uq, up, NTD)
    s_neg = score_scale * dot3(uq, un, NTD)
    lanes = lax.broadcasted_iota(jnp.int32, (ALL, ALL), 1)
    diag = lax.broadcasted_iota(jnp.int32, (ALL, ALL), 0) == lanes
    all_ids = L[0, :, 3, 0:128].astype(jnp.int32)
    named = lanes == all_ids[:, 0:1]
    for k in range(1, NEGS):
        named = jnp.logical_or(named, lanes == all_ids[:, k : k + 1])
    ex_in = jnp.exp(s_in)
    ex_neg = jnp.where(named, jnp.exp(s_neg), 0.0)
    total = jnp.sum(ex_in, 1, keepdims=True) + jnp.sum(ex_neg, 1, keepdims=True)
    own_score = jnp.sum(jnp.where(diag, s_in, 0.0), 1, keepdims=True)
    loss_ref[...] = jnp.sum(jnp.log(total) - own_score, 0, keepdims=True) / ALL
    factor = (score_scale * loss_scale) / total
    g_in = ex_in * factor - jnp.where(diag, score_scale * loss_scale, 0.0)
    g_neg = ex_neg * factor
    turn = next_turn(turn, 8)
    d_uq = dot3(split2(g_in), up) + dot3(split2(g_neg), un)
    d_up = dot3(split2(g_in.T), uq)
    d_un = dot3(split2(g_neg.T), uq)
    d_unit = jnp.concatenate([d_uq, d_up, d_un], 0)
    dproj[...] = (d_unit - unit * jnp.sum(unit * d_unit, -1, keepdims=True)) * r_norm

    own_rows[...] = jnp.zeros_like(own_rows)
    for s in range(SLOTS):
        for k in range(KINDS):
            own_rows[4 * s + k : 4 * s + k + 1, :] = dproj[pl.ds(k * ALL + s * DP + dp, 1), :]
    d_pooled = join3(dot(split3(own_rows[...]), w_ref[...], NTD))
    lifted = d_pooled * gain
    spread = join3(dot(split3(lifted), xs[...], NTD))
    dot_own[...] = jnp.sum(jnp.where(mine, spread, 0.0), 0, keepdims=True)
    for cp in turn:
        cp.wait()
    dots = tensor_sum(dot_own, dot_land, s_dot, r_dot)

    inner = scales * scales / D * dots
    rows = jnp.concatenate([coeffs, coeffs * inner, jnp.zeros((6, TOK), f32)], 0)
    cols = rows.T
    for i in range(KINDS):
        for s in range(SLOTS):
            at = (i * SLOTS + s) * LEN
            value = cols[at : at + LEN, 0:1] * lifted[4 * s + i : 4 * s + i + 1, :] - (
                xs[pl.ds(at, LEN), :].astype(f32) * cols[at : at + LEN, 1:2]
            )
            g_refs[i][pl.ds(s * LEN, LEN), :] = value.astype(bf16)

    plain_all = jnp.concatenate(
        [
            jnp.concatenate([PB[i, :, 4 * s + k, :] for i in range(NX)], 0)
            for k in range(KINDS)
            for s in range(SLOTS)
        ],
        0,
    )
    grad = dot3(split2(plain_all.T), split2(dproj[...])) / loss_scale
    gg_ref[...] = exact_dot(jnp.ones((8, E), f32), grad * w_ref[...].astype(f32), NTD)[0:1]
    gw_ref[...] = (grad * gain.T).astype(bf16)


def body(q, p, n, q_len, p_len, n_len, gain, w, owner, slot):
    vmem = pl.BlockSpec(memory_space=pltpu.VMEM)
    smem = pl.BlockSpec(memory_space=pltpu.SMEM)
    dma = pltpu.SemaphoreType.DMA
    states = [v.reshape(SLOTS * LEN, F) for v in (q, p, n)]

    def run(x0, x1, x2, l0, l1, l2, gain_ref, w_ref, owner_ref, slot_ref, g0, g1, g2, *rest):
        kernel((x0, x1, x2), (l0, l1, l2), gain_ref, w_ref, owner_ref, slot_ref, (g0, g1, g2), *rest)

    state_out = jax.ShapeDtypeStruct((SLOTS * LEN, F), bf16)
    g0, g1, g2, gw, gg, loss = pl.pallas_call(
        run,
        out_shape=(
            state_out,
            state_out,
            state_out,
            jax.ShapeDtypeStruct((F, E), bf16),
            jax.ShapeDtypeStruct((1, F), f32),
            jax.ShapeDtypeStruct((1, 1), f32),
        ),
        in_specs=[vmem] * 3 + [smem] * 3 + [vmem] * 4,
        out_specs=(vmem,) * 6,
        scratch_shapes=[
            pltpu.VMEM((TOK, F), bf16),
            pltpu.VMEM((1, TOK), f32),
            pltpu.VMEM((NT, 1, TOK), f32),
            pltpu.VMEM((1, TOK), f32),
            pltpu.VMEM((NT, 1, TOK), f32),
            pltpu.VMEM((NT, 4, H), f32),
            pltpu.VMEM((NT, 4, H), f32),
            pltpu.VMEM((SLOTS, 1, H), f32),
            pltpu.VMEM((NC, ALL, 4, H), f32),
            pltpu.VMEM((NX, NZ, 16, F), f32),
            pltpu.VMEM((SEQ, E), bf16),
            pltpu.VMEM((SEQ, E), bf16),
            pltpu.VMEM((SEQ, E), f32),
            pltpu.VMEM((16, E), f32),
            dma((NT - 1,)),
            dma((NT - 1,)),
            dma((NT - 1,)),
            dma((NT - 1,)),
            dma((NZ - 1,)),
            dma((NZ - 1,)),
            dma((3,)),
            dma((3,)),
            dma((3,)),
            dma((3,)),
            dma((4,)),
            dma((4,)),
            dma((NT - 1,)),
            dma((NT - 1,)),
            dma((3,)),
            dma((3,)),
            dma((2, 8)),
            dma((2, 8)),
        ],
        compiler_params=pltpu.CompilerParams(
            collective_id=0, has_side_effects=True, vmem_limit_bytes=50 << 20
        ),
    )(*states, q_len, p_len, n_len, gain.reshape(1, F), w, owner, slot)
    shape = q.shape
    return (
        g0.reshape(shape),
        g1.reshape(shape),
        g2.reshape(shape),
        gw,
        gg.reshape(F),
        loss.reshape(()),
    )


def solution(mesh):
    placed = (
        P("dp", None, "tensor"),
        P("dp", None, "tensor"),
        P("dp", None, "tensor"),
        P("dp"),
        P("dp"),
        P("dp"),
        P("tensor"),
        P("tensor", None),
        P("dp", None),
        P("dp", None),
    )
    return jax.shard_map(
        body,
        mesh=mesh,
        in_specs=placed,
        out_specs=(
            P("dp", None, "tensor"),
            P("dp", None, "tensor"),
            P("dp", None, "tensor"),
            P("tensor", None),
            P("tensor"),
            P(),
        ),
        check_vma=False,
    )
```

```python
import jax
import jax.numpy as jnp
from jax import lax
from jax.experimental import pallas as pl
from jax.experimental.pallas import tpu as pltpu
from jax.sharding import PartitionSpec as P

NX, NY, NZ, NC = 4, 4, 16, 2
NT = NY * NC
DP = NX * NZ
D = 4096
F = D // NT
E = 768
H = E // NC
LEN = 64
SLOTS = 4
NEGS = 7
KINDS = 3
TOK = KINDS * SLOTS * LEN
ALL = SLOTS * DP
SEQ = KINDS * ALL
score_scale = 20.0
loss_scale = 1024.0
epsilon = 1e-06
MESH = pl.DeviceIdType.MESH
f32 = jnp.float32
bf16 = jnp.bfloat16
NN = (((1,), (0,)), ((), ()))
NTD = (((1,), (1,)), ((), ()))
TN = (((0,), (0,)), ((), ()))


def dot(a, b, dims=NN):
    return lax.dot_general(a, b, dims, preferred_element_type=f32)


def exact_dot(a, b, dims=NN):
    return lax.dot_general(a, b, dims, preferred_element_type=f32, precision=lax.Precision.HIGHEST)


def split2(v):
    hi = v.astype(bf16)
    return hi, (v - hi.astype(f32)).astype(bf16)


def split3(v):
    hi = v.astype(bf16)
    rest = v - hi.astype(f32)
    mid = rest.astype(bf16)
    return jnp.concatenate([hi, mid, (rest - mid.astype(f32)).astype(bf16)], 0)


def join3(v):
    return v[0:16] + v[16:32] + v[32:48]


def dot3(a, b, dims=NN):
    return dot(a[0], b[0], dims) + (dot(a[0], b[1], dims) + dot(a[1], b[0], dims))


def kernel(
    x_hbm,
    len_hbm,
    gain_hbm,
    w_hbm,
    owner_hbm,
    slot_hbm,
    lifted_hbm,
    factors_hbm,
    gw_hbm,
    gg_hbm,
    loss_hbm,
    xs,
    lifted_ref,
    factors_ref,
    gw_ref,
    gg_ref,
    loss_ref,
    s_out_copy,
    len_ref,
    gain_ref,
    w_ref,
    owner_ref,
    slot_ref,
    s_in_copy,
    sq_own,
    sq_land,
    dot_own,
    dot_land,
    stage,
    rs_land,
    ids_ref,
    L,
    PB,
    u_hi,
    u_lo,
    dproj,
    own_rows,
    s_sq,
    r_sq,
    s_rs,
    r_rs,
    s_z,
    r_z,
    s_a,
    r_a,
    s_b,
    r_b,
    s_c,
    r_c,
    s_dot,
    r_dot,
    s_px,
    r_px,
    s_pz,
    r_pz,
):
    dp = lax.axis_index("dp")
    t = lax.axis_index("tensor")
    x, z = dp // NZ, dp % NZ
    y, c = t // NC, t % NC
    a = jnp.where(c == 0, x, y)
    b = jnp.where(c == 0, y, x)

    def tensor_peer(k):
        return (dp, (t + k) % NT)

    def x_peer(k):
        return (((x + k) % NX) * NZ + z, t)

    def y_peer(k):
        return (dp, ((y + k) % NY) * NC + c)

    def z_peer(k):
        return (x * NZ + (z + k) % NZ, t)

    def either(cond, p, q):
        return tuple(jnp.where(cond, i, j) for i, j in zip(p, q))

    def a_peer(k):
        return either(c == 0, x_peer(k), y_peer(k))

    def b_peer(k):
        return either(c == 0, y_peer(k), x_peer(k))

    sibling = (dp, y * NC + 1 - c)

    def send(src, dst, ss, rs, to):
        cp = pltpu.make_async_remote_copy(
            src_ref=src, dst_ref=dst, send_sem=ss, recv_sem=rs, device_id=to, device_id_type=MESH
        )
        cp.start()
        return cp

    loads = []

    def load(src, dst):
        cp = pltpu.make_async_copy(src, dst, s_in_copy.at[len(loads)])
        cp.start()
        loads.append(cp)

    for i in range(KINDS):
        load(x_hbm[i], xs.at[pl.ds(i * SLOTS * LEN, SLOTS * LEN), :])
    for i in range(KINDS):
        load(len_hbm[i], len_ref.at[i])
    load(gain_hbm, gain_ref)
    load(owner_hbm, owner_ref)
    load(slot_hbm, slot_ref)
    load(w_hbm, w_ref)

    stores = []

    def store(src, dst):
        cp = pltpu.make_async_copy(src, dst, s_out_copy.at[len(stores)])
        cp.start()
        stores.append(cp)

    barrier = pltpu.get_barrier_semaphore()
    greeted = (
        [tensor_peer(k) for k in range(1, NT)]
        + [x_peer(k) for k in range(1, NX)]
        + [z_peer(k) for k in range(1, NZ)]
    )
    for peer in greeted:
        pl.semaphore_signal(barrier, inc=1, device_id=peer, device_id_type=MESH)

    for cp in loads[:KINDS]:
        cp.wait()
    xf = xs[...].astype(f32)
    xf = xf * xf
    part = (xf[:, 0:128] + xf[:, 128:256]) + (xf[:, 256:384] + xf[:, 384:512])
    sq_own[...] = exact_dot(jnp.ones((8, 128), f32), part, NTD)[0:1]

    for cp in loads[KINDS:]:
        cp.wait()
    pl.semaphore_wait(barrier, len(greeted))

    def tensor_send(own, land, ss, rs):
        cps = [send(own, land.at[t], ss.at[k - 1], rs.at[k - 1], tensor_peer(k)) for k in range(1, NT)]
        land[t] = own[...]
        return cps

    def tensor_sum(cps, land):
        for cp in cps:
            cp.wait()
        total = land[0]
        for i in range(1, NT):
            total = total + land[i]
        return total

    squares = tensor_sum(tensor_send(sq_own, sq_land, s_sq, r_sq), sq_land)
    scales = lax.rsqrt(squares / D + epsilon)
    lane = lax.broadcasted_iota(jnp.int32, (1, TOK), 1)
    seq = lane // LEN
    lens = jnp.zeros((1, TOK), jnp.int32)
    for i in range(KINDS):
        for s in range(SLOTS):
            lens = jnp.where(seq == i * SLOTS + s, len_ref[i, s], lens)
    live = jnp.where(lane % LEN < lens, 1.0 / lens.astype(f32), 0.0)
    coeffs = scales * live
    row = lax.broadcasted_iota(jnp.int32, (16, TOK), 0)
    mine = (row % 4) * SLOTS + row // 4 == seq
    plain = join3(dot(split3(jnp.where(mine, coeffs, 0.0)), xs[...]))
    for s in range(SLOTS):
        for k in range(KINDS):
            PB[x, z, k, s : s + 1, :] = plain[4 * s + k : 4 * s + k + 1]
    px = [
        send(PB.at[x, z], PB.at[x, z], s_px.at[k - 1], r_px.at[k - 1], x_peer(k))
        for k in range(1, NX)
    ]
    gain = gain_ref[...]
    proj = join3(dot(split3(plain * gain), w_ref[...]))
    for s in range(SLOTS):
        for h in range(NC):
            stage[s * NC + h] = proj[4 * s : 4 * s + 4, h * H : (h + 1) * H]
    cps = [
        send(stage.at[(t + k) % NT], rs_land.at[t], s_rs.at[k - 1], r_rs.at[k - 1], tensor_peer(k))
        for k in range(1, NT)
    ]
    rs_land[t] = stage[t]
    ids = (slot_ref[...] * DP + owner_ref[...]).astype(f32)
    ids_ref[...] = jnp.zeros_like(ids_ref)
    for s in range(SLOTS):
        ids_ref[s, :, 0:NEGS] = ids[s : s + 1]
    for cp in cps:
        cp.wait()
    piece = rs_land[0]
    for i in range(1, NT):
        piece = piece + rs_land[i]
    place = lax.broadcasted_iota(jnp.int32, (4, H), 0)
    L[c, 0, b, a, 4] = jnp.where(place == 3, ids_ref[y], piece)
    mine_block = L.at[c, 0, b, a, 4]

    zs = {}
    for k in (8, 9, 7, 10, 6, 11, 5, 12, 4, 13, 3, 14, 2, 15, 1):
        rel = (4 - k) % NZ
        zs[rel] = send(mine_block, L.at[c, rel // 8, b, a, rel % 8], s_z.at[k - 1], r_z.at[k - 1], z_peer(k))

    for cp in px:
        cp.wait()

    def ring(step):
        out = []
        if step <= 8:
            up = PB.at[:, (z - step + 1 + NZ) % NZ]
            out.append(send(up, up, s_pz.at[0, step - 1], r_pz.at[0, step - 1], z_peer(1)))
        if step <= 7:
            down = PB.at[:, (z + step - 1) % NZ]
            out.append(send(down, down, s_pz.at[1, step - 1], r_pz.at[1, step - 1], z_peer(NZ - 1)))
        return out

    def next_turn(turn, step):
        for cp in turn:
            cp.wait()
        return ring(step)

    def along_a(g):
        line = L.at[c, g, b, a]
        return [send(line, line, s_a.at[g, k - 1], r_a.at[g, k - 1], a_peer(k)) for k in (2, 1, 3)]

    def along_b(g):
        plane = L.at[c, g, b]
        cps = [send(plane, plane, s_b.at[g, k - 1], r_b.at[g, k - 1], b_peer(k)) for k in (2, 1, 3)]
        return cps, send(plane, plane, s_c.at[g, 0], r_c.at[g, 0], sibling)

    def across(g, k):
        got = L.at[c, g, (b + 4 - k) % 4]
        return send(got, got, s_c.at[g, k], r_c.at[g, k], sibling)

    turn = ring(1)
    for rel in (5, 3, 6, 2, 7, 1, 0):
        zs[rel].wait()
    a0 = along_a(0)
    turn = next_turn(turn, 2)
    for rel in range(8, 16):
        zs[rel].wait()
    a1 = along_a(1)
    for cp in a0:
        cp.wait()
    b0, over = along_b(0)
    crossing = [over]
    turn = next_turn(turn, 3)
    for cp in a1:
        cp.wait()
    b1, over = along_b(1)
    crossing.append(over)
    turn = next_turn(turn, 4)
    for k in (1, 3, 2):
        b0[(2, 1, 3).index(k)].wait()
        crossing.append(across(0, k))
    turn = next_turn(turn, 5)
    for k in (1, 3, 2):
        b1[(2, 1, 3).index(k)].wait()
        crossing.append(across(1, k))
    turn = next_turn(turn, 6)
    for cp in crossing:
        cp.wait()
    turn = next_turn(turn, 7)

    shift = (z + NZ - 4) % NZ
    for k in range(KINDS):
        for s in range(SLOTS):
            for i in range(NX):
                left = jnp.concatenate([L[0, g, s, i, :, k, :] for g in range(2)], 0)
                right = jnp.concatenate([L[1, g, i, s, :, k, :] for g in range(2)], 0)
                rows = pl.ds(k * ALL + s * DP + i * NZ, NZ)
                dproj[rows, :] = pltpu.roll(jnp.concatenate([left, right], 1), shift, 0)
    projs = dproj[...]
    r_norm = lax.rsqrt(jnp.sum(projs * projs, -1, keepdims=True) + epsilon)
    unit = projs * r_norm
    hi, lo = split2(unit)
    u_hi[...] = hi
    u_lo[...] = lo
    turn = next_turn(turn, 8)

    def part_of(k):
        rows = pl.ds(k * ALL, ALL)
        return u_hi[rows, :], u_lo[rows, :]

    uq, up, un = part_of(0), part_of(1), part_of(2)
    s_in = score_scale * dot3(uq, up, NTD)
    s_neg = score_scale * dot3(uq, un, NTD)
    lanes = lax.broadcasted_iota(jnp.int32, (ALL, ALL), 1)
    diag = lax.broadcasted_iota(jnp.int32, (ALL, ALL), 0) == lanes
    all_ids = jnp.concatenate(
        [
            pltpu.roll(jnp.concatenate([L[0, g, s, i, :, 3, 0:128] for g in range(2)], 0), shift, 0)
            for s in range(SLOTS)
            for i in range(NX)
        ],
        0,
    ).astype(jnp.int32)
    named = lanes == all_ids[:, 0:1]
    for k in range(1, NEGS):
        named = jnp.logical_or(named, lanes == all_ids[:, k : k + 1])
    ex_in = jnp.exp(s_in)
    ex_neg = jnp.where(named, jnp.exp(s_neg), 0.0)
    total = jnp.sum(ex_in, 1, keepdims=True) + jnp.sum(ex_neg, 1, keepdims=True)
    own_score = jnp.sum(jnp.where(diag, s_in, 0.0), 1, keepdims=True)
    loss_ref[...] = jnp.sum(jnp.log(total) - own_score, 0, keepdims=True) / ALL
    store(loss_ref, loss_hbm)
    factor = (score_scale * loss_scale) / total
    g_in = ex_in * factor - jnp.where(diag, score_scale * loss_scale, 0.0)
    g_neg = ex_neg * factor
    d_uq = dot3(split2(g_in), up) + dot3(split2(g_neg), un)
    d_up = dot3(split2(g_in.T), uq)
    d_un = dot3(split2(g_neg.T), uq)
    d_unit = jnp.concatenate([d_uq, d_up, d_un], 0)
    dproj[...] = (d_unit - unit * jnp.sum(unit * d_unit, -1, keepdims=True)) * r_norm

    own_rows[...] = jnp.zeros_like(own_rows)
    for s in range(SLOTS):
        for k in range(KINDS):
            own_rows[4 * s + k : 4 * s + k + 1, :] = dproj[pl.ds(k * ALL + s * DP + dp, 1), :]
    d_pooled = join3(dot(split3(own_rows[...]), w_ref[...], NTD))
    lifted = d_pooled * gain
    lifted_ref[...] = lifted
    store(lifted_ref, lifted_hbm)
    spread = join3(dot(split3(lifted), xs[...], NTD))
    dot_own[...] = jnp.sum(jnp.where(mine, spread, 0.0), 0, keepdims=True)
    dots_sent = tensor_send(dot_own, dot_land, s_dot, r_dot)
    for cp in turn:
        cp.wait()

    plain_all = jnp.concatenate(
        [
            PB[i, :, k, s, :]
            for k in range(KINDS)
            for s in range(SLOTS)
            for i in range(NX)
        ],
        0,
    )
    grad = dot3(split2(plain_all), split2(dproj[...]), TN) / loss_scale
    weighted = grad * w_ref[...].astype(f32)
    fold = weighted[:, 0:128]
    for i in range(1, E // 128):
        fold = fold + weighted[:, i * 128 : (i + 1) * 128]
    gg_ref[...] = exact_dot(jnp.ones((8, 128), f32), fold, NTD)[0:1]
    gw_ref[...] = (grad * gain.T).astype(bf16)
    store(gg_ref, gg_hbm)
    store(gw_ref, gw_hbm)

    dots = tensor_sum(dots_sent, dot_land)

    inner = scales * scales / D * dots
    factors_ref[...] = jnp.concatenate([coeffs, coeffs * inner, jnp.zeros((6, TOK), f32)], 0)
    store(factors_ref, factors_hbm)
    for cp in stores:
        cp.wait()


def finish_kernel(*refs):
    x_hbm, (lifted_hbm, factors_hbm, gw_in, gg_in, loss_in) = refs[0:3], refs[3:8]
    g_hbm, (gw_out, gg_out, loss_out) = refs[8:11], refs[11:14]
    xs, gs, lifted_ref, factors_ref, gw_ref, gg_ref, loss_ref, s_load, s_store = refs[14:]

    def copy(src, dst, sem):
        cp = pltpu.make_async_copy(src, dst, sem)
        cp.start()
        return cp

    def part(ref, i):
        return ref.at[pl.ds(i * SLOTS * LEN, SLOTS * LEN), :]

    first = [copy(factors_hbm, factors_ref, s_load.at[0]), copy(lifted_hbm, lifted_ref, s_load.at[1])]
    states = [copy(x_hbm[i], part(xs, i), s_load.at[2 + i]) for i in range(KINDS)]
    passed = [
        (copy(src, mid, s_load.at[5 + i]), mid, dst)
        for i, (src, mid, dst) in enumerate(
            ((gw_in, gw_ref, gw_out), (gg_in, gg_ref, gg_out), (loss_in, loss_ref, loss_out))
        )
    ]
    for cp in first:
        cp.wait()
    cols = factors_ref[...].T
    stores = []
    for i in range(KINDS):
        states[i].wait()
        for s in range(SLOTS):
            at = (i * SLOTS + s) * LEN
            value = cols[at : at + LEN, 0:1] * lifted_ref[4 * s + i : 4 * s + i + 1, :] - (
                xs[pl.ds(at, LEN), :].astype(f32) * cols[at : at + LEN, 1:2]
            )
            gs[pl.ds(at, LEN), :] = value.astype(bf16)
        stores.append(copy(part(gs, i), g_hbm[i], s_store.at[i]))
        cp, mid, dst = passed[i]
        cp.wait()
        stores.append(copy(mid, dst, s_store.at[KINDS + i]))
    for cp in stores:
        cp.wait()


def body(q, p, n, q_len, p_len, n_len, gain, w, owner, slot):
    hbm = pl.BlockSpec(memory_space=pltpu.HBM)
    dma = pltpu.SemaphoreType.DMA
    states = [v.reshape(SLOTS * LEN, F) for v in (q, p, n)]

    def run(x0, x1, x2, l0, l1, l2, *rest):
        kernel((x0, x1, x2), (l0, l1, l2), *rest)

    state_out = jax.ShapeDtypeStruct((SLOTS * LEN, F), bf16)
    results = pl.pallas_call(
        run,
        out_shape=(
            jax.ShapeDtypeStruct((16, F), f32),
            jax.ShapeDtypeStruct((8, TOK), f32),
            jax.ShapeDtypeStruct((F, E), bf16),
            jax.ShapeDtypeStruct((1, F), f32),
            jax.ShapeDtypeStruct((1, 1), f32),
        ),
        in_specs=[hbm] * 10,
        out_specs=(hbm,) * 5,
        scratch_shapes=[
            pltpu.VMEM((TOK, F), bf16),
            pltpu.VMEM((16, F), f32),
            pltpu.VMEM((8, TOK), f32),
            pltpu.VMEM((F, E), bf16),
            pltpu.VMEM((1, F), f32),
            pltpu.VMEM((1, 1), f32),
            dma((5,)),
            pltpu.SMEM((KINDS, SLOTS), jnp.int32),
            pltpu.VMEM((1, F), f32),
            pltpu.VMEM((F, E), bf16),
            pltpu.VMEM((SLOTS, NEGS), jnp.int32),
            pltpu.VMEM((SLOTS, NEGS), jnp.int32),
            dma((10,)),
            pltpu.VMEM((1, TOK), f32),
            pltpu.VMEM((NT, 1, TOK), f32),
            pltpu.VMEM((1, TOK), f32),
            pltpu.VMEM((NT, 1, TOK), f32),
            pltpu.VMEM((NT, 4, H), f32),
            pltpu.VMEM((NT, 4, H), f32),
            pltpu.VMEM((SLOTS, 1, H), f32),
            pltpu.VMEM((NC, 2, 4, 4, 8, 4, H), f32),
            pltpu.VMEM((NX, NZ, KINDS, SLOTS, F), f32),
            pltpu.VMEM((SEQ, E), bf16),
            pltpu.VMEM((SEQ, E), bf16),
            pltpu.VMEM((SEQ, E), f32),
            pltpu.VMEM((16, E), f32),
            dma((NT - 1,)),
            dma((NT - 1,)),
            dma((NT - 1,)),
            dma((NT - 1,)),
            dma((NZ - 1,)),
            dma((NZ - 1,)),
            dma((2, 3)),
            dma((2, 3)),
            dma((2, 3)),
            dma((2, 3)),
            dma((2, 4)),
            dma((2, 4)),
            dma((NT - 1,)),
            dma((NT - 1,)),
            dma((3,)),
            dma((3,)),
            dma((2, 8)),
            dma((2, 8)),
        ],
        compiler_params=pltpu.CompilerParams(
            collective_id=0, has_side_effects=True, vmem_limit_bytes=62 << 20
        ),
    )(*states, q_len, p_len, n_len, gain.reshape(1, F), w, owner, slot)
    g0, g1, g2, gw, gg, loss = pl.pallas_call(
        finish_kernel,
        out_shape=(state_out,) * 3 + tuple(jax.ShapeDtypeStruct(v.shape, v.dtype) for v in results[2:]),
        in_specs=[hbm] * 8,
        out_specs=(hbm,) * 6,
        scratch_shapes=[
            pltpu.VMEM((TOK, F), bf16),
            pltpu.VMEM((TOK, F), bf16),
            pltpu.VMEM((16, F), f32),
            pltpu.VMEM((8, TOK), f32),
            pltpu.VMEM((F, E), bf16),
            pltpu.VMEM((1, F), f32),
            pltpu.VMEM((1, 1), f32),
            dma((8,)),
            dma((6,)),
        ],
        compiler_params=pltpu.CompilerParams(vmem_limit_bytes=62 << 20),
    )(*states, *results)
    shape = q.shape
    return (
        g0.reshape(shape),
        g1.reshape(shape),
        g2.reshape(shape),
        gw,
        gg.reshape(F),
        loss.reshape(()),
    )


def solution(mesh):
    placed = (
        P("dp", None, "tensor"),
        P("dp", None, "tensor"),
        P("dp", None, "tensor"),
        P("dp"),
        P("dp"),
        P("dp"),
        P("tensor"),
        P("tensor", None),
        P("dp", None),
        P("dp", None),
    )
    return jax.shard_map(
        body,
        mesh=mesh,
        in_specs=placed,
        out_specs=(
            P("dp", None, "tensor"),
            P("dp", None, "tensor"),
            P("dp", None, "tensor"),
            P("tensor", None),
            P("tensor"),
            P(),
        ),
        check_vma=False,
    )
```

```python
import jax
import jax.numpy as jnp
from jax import lax
from jax.experimental import pallas as pl
from jax.experimental.pallas import tpu as pltpu
from jax.sharding import PartitionSpec as P

NX, NY, NZ, NC = 4, 4, 16, 2
NT = NY * NC
DP = NX * NZ
D = 4096
F = D // NT
E = 768
H = E // NC
LEN = 64
SLOTS = 4
NEGS = 7
KINDS = 3
TOK = KINDS * SLOTS * LEN
ALL = SLOTS * DP
SEQ = KINDS * ALL
score_scale = 20.0
loss_scale = 1024.0
epsilon = 1e-06
MESH = pl.DeviceIdType.MESH
f32 = jnp.float32
bf16 = jnp.bfloat16
NN = (((1,), (0,)), ((), ()))
NTD = (((1,), (1,)), ((), ()))
TN = (((0,), (0,)), ((), ()))


def dot(a, b, dims=NN):
    return lax.dot_general(a, b, dims, preferred_element_type=f32)


def exact_dot(a, b, dims=NN):
    return lax.dot_general(a, b, dims, preferred_element_type=f32, precision=lax.Precision.HIGHEST)


def split2(v):
    hi = v.astype(bf16)
    return hi, (v - hi.astype(f32)).astype(bf16)


def split3(v):
    hi = v.astype(bf16)
    rest = v - hi.astype(f32)
    mid = rest.astype(bf16)
    return jnp.concatenate([hi, mid, (rest - mid.astype(f32)).astype(bf16)], 0)


def join3(v):
    return v[0:16] + v[16:32] + v[32:48]


def dot3(a, b, dims=NN):
    return dot(a[0], b[0], dims) + (dot(a[0], b[1], dims) + dot(a[1], b[0], dims))


def kernel(
    x_hbm,
    len_hbm,
    gain_hbm,
    w_hbm,
    owner_hbm,
    slot_hbm,
    lifted_hbm,
    factors_hbm,
    gw_hbm,
    gg_hbm,
    loss_hbm,
    xs,
    lifted_ref,
    factors_ref,
    gw_ref,
    gg_ref,
    loss_ref,
    s_out_copy,
    len_ref,
    gain_ref,
    w_ref,
    owner_ref,
    slot_ref,
    s_in_copy,
    sq_own,
    sq_land,
    dot_own,
    dot_land,
    stage,
    rs_land,
    ids_ref,
    L,
    PB,
    u_hi,
    u_lo,
    dproj,
    parts,
    own_rows,
    s_sq,
    r_sq,
    s_rs,
    r_rs,
    s_z,
    r_z,
    s_a,
    r_a,
    s_b,
    r_b,
    s_c,
    r_c,
    s_dot,
    r_dot,
    s_px,
    r_px,
    s_pz,
    r_pz,
):
    dp = lax.axis_index("dp")
    t = lax.axis_index("tensor")
    x, z = dp // NZ, dp % NZ
    y, c = t // NC, t % NC
    a = jnp.where(c == 0, x, y)
    b = jnp.where(c == 0, y, x)

    def tensor_peer(k):
        return (dp, (t + k) % NT)

    def x_peer(k):
        return (((x + k) % NX) * NZ + z, t)

    def y_peer(k):
        return (dp, ((y + k) % NY) * NC + c)

    def z_peer(k):
        return (x * NZ + (z + k) % NZ, t)

    def either(cond, p, q):
        return tuple(jnp.where(cond, i, j) for i, j in zip(p, q))

    def a_peer(k):
        return either(c == 0, x_peer(k), y_peer(k))

    def b_peer(k):
        return either(c == 0, y_peer(k), x_peer(k))

    sibling = (dp, y * NC + 1 - c)

    def send(src, dst, ss, rs, to):
        cp = pltpu.make_async_remote_copy(
            src_ref=src, dst_ref=dst, send_sem=ss, recv_sem=rs, device_id=to, device_id_type=MESH
        )
        cp.start()
        return cp

    loads = []

    def load(src, dst):
        cp = pltpu.make_async_copy(src, dst, s_in_copy.at[len(loads)])
        cp.start()
        loads.append(cp)

    for i in range(KINDS):
        load(x_hbm[i], xs.at[pl.ds(i * SLOTS * LEN, SLOTS * LEN), :])
    for i in range(KINDS):
        load(len_hbm[i], len_ref.at[i])
    load(gain_hbm, gain_ref)
    load(owner_hbm, owner_ref)
    load(slot_hbm, slot_ref)
    load(w_hbm, w_ref)

    stores = []

    def store(src, dst):
        cp = pltpu.make_async_copy(src, dst, s_out_copy.at[len(stores)])
        cp.start()
        stores.append(cp)

    barrier = pltpu.get_barrier_semaphore()
    greeted = (
        [tensor_peer(k) for k in range(1, NT)]
        + [x_peer(k) for k in range(1, NX)]
        + [z_peer(k) for k in range(1, NZ)]
    )
    for peer in greeted:
        pl.semaphore_signal(barrier, inc=1, device_id=peer, device_id_type=MESH)

    for cp in loads[:KINDS]:
        cp.wait()
    xf = xs[...].astype(f32)
    xf = xf * xf
    part = (xf[:, 0:128] + xf[:, 128:256]) + (xf[:, 256:384] + xf[:, 384:512])
    sq_own[...] = exact_dot(jnp.ones((8, 128), f32), part, NTD)[0:1]

    for cp in loads[KINDS:]:
        cp.wait()
    pl.semaphore_wait(barrier, len(greeted))

    def tensor_send(own, land, ss, rs):
        cps = [send(own, land.at[t], ss.at[k - 1], rs.at[k - 1], tensor_peer(k)) for k in range(1, NT)]
        land[t] = own[...]
        return cps

    def tensor_sum(cps, land):
        for cp in cps:
            cp.wait()
        total = land[0]
        for i in range(1, NT):
            total = total + land[i]
        return total

    squares = tensor_sum(tensor_send(sq_own, sq_land, s_sq, r_sq), sq_land)
    scales = lax.rsqrt(squares / D + epsilon)
    lane = lax.broadcasted_iota(jnp.int32, (1, TOK), 1)
    seq = lane // LEN
    lens = jnp.zeros((1, TOK), jnp.int32)
    for i in range(KINDS):
        for s in range(SLOTS):
            lens = jnp.where(seq == i * SLOTS + s, len_ref[i, s], lens)
    live = jnp.where(lane % LEN < lens, 1.0 / lens.astype(f32), 0.0)
    coeffs = scales * live
    row = lax.broadcasted_iota(jnp.int32, (16, TOK), 0)
    mine = (row % 4) * SLOTS + row // 4 == seq
    plain = join3(dot(split3(jnp.where(mine, coeffs, 0.0)), xs[...]))
    for s in range(SLOTS):
        for k in range(KINDS):
            PB[0, x, 4, k, s : s + 1, :] = plain[4 * s + k : 4 * s + k + 1]
    gain = gain_ref[...]
    proj = join3(dot(split3(plain * gain), w_ref[...]))
    for s in range(SLOTS):
        for h in range(NC):
            stage[s * NC + h] = proj[4 * s : 4 * s + 4, h * H : (h + 1) * H]
    cps = [
        send(stage.at[(t + k) % NT], rs_land.at[t], s_rs.at[k - 1], r_rs.at[k - 1], tensor_peer(k))
        for k in range(1, NT)
    ]
    rs_land[t] = stage[t]

    def pz_send(ks):
        block = PB.at[0, x, 4]
        out = []
        for k in ks:
            rel = (4 - k) % NZ
            out.append(send(block, PB.at[rel // 8, x, rel % 8], s_pz.at[k - 1], r_pz.at[k - 1], z_peer(k)))
        return out

    pz0 = pz_send((4, 3, 13, 2, 14, 1, 15))
    ids = (slot_ref[...] * DP + owner_ref[...]).astype(f32)
    ids_ref[...] = jnp.zeros_like(ids_ref)
    for s in range(SLOTS):
        ids_ref[s, :, 0:NEGS] = ids[s : s + 1]
    for cp in cps:
        cp.wait()
    piece = rs_land[0]
    for i in range(1, NT):
        piece = piece + rs_land[i]
    place = lax.broadcasted_iota(jnp.int32, (4, H), 0)
    L[c, 0, b, a, 4] = jnp.where(place == 3, ids_ref[y], piece)
    mine_block = L.at[c, 0, b, a, 4]

    zs = {}
    for k in (8, 9, 7, 10, 6, 11, 5, 12, 4, 13, 3, 14, 2, 15, 1):
        rel = (4 - k) % NZ
        zs[rel] = send(mine_block, L.at[c, rel // 8, b, a, rel % 8], s_z.at[k - 1], r_z.at[k - 1], z_peer(k))

    def px_send(g, i, block, k):
        return send(block, block, s_px.at[g, i], r_px.at[g, i], x_peer(k))

    def px_start(g, pz):
        for cp in pz:
            cp.wait()
        return [px_send(g, 0, PB.at[g, x], 1), px_send(g, 1, PB.at[g, x], 3)]

    def px_relay(g, cps):
        cps[0].wait()
        cps.append(px_send(g, 2, PB.at[g, (x + 3) % NX, pl.ds(0, 4)], 1))
        cps[1].wait()
        cps.append(px_send(g, 3, PB.at[g, (x + 1) % NX, pl.ds(4, 4)], 3))

    def along_a(g):
        line = L.at[c, g, b, a]
        return [send(line, line, s_a.at[g, k - 1], r_a.at[g, k - 1], a_peer(k)) for k in (2, 1, 3)]

    def half(g, k, h):
        return L.at[c, g, (b + k) % 4, pl.ds(2 * h, 2)]

    def b_send(g, i, block, k):
        return send(block, block, s_b.at[g, i], r_b.at[g, i], b_peer(k))

    def cross(g, k):
        plane = L.at[c, g, (b + k) % 4]
        return send(plane, plane, s_c.at[g, k], r_c.at[g, k], sibling)

    def b_start(g):
        cps = [
            b_send(g, 0, half(g, 0, 0), 1),
            b_send(g, 1, half(g, 0, 1), 3),
            b_send(g, 2, half(g, 0, 1), 1),
            b_send(g, 3, half(g, 0, 0), 3),
        ]
        return cps, [cross(g, 0)]

    def b_relay(g, cps):
        cps[0].wait()
        cps.append(b_send(g, 4, half(g, 3, 0), 1))
        cps[1].wait()
        cps.append(b_send(g, 5, half(g, 1, 1), 3))

    def b_middle(g, cps, over):
        cps[2].wait()
        over.append(cross(g, 3))
        cps[3].wait()
        over.append(cross(g, 1))

    def b_end(g, cps, over):
        cps[4].wait()
        cps[5].wait()
        over.append(cross(g, 2))

    px0 = px_start(0, pz0)
    for rel in (5, 3, 6, 2, 7, 1, 0):
        zs[rel].wait()
    a0 = along_a(0)
    pz1 = pz_send((8, 9, 7, 10, 6, 11, 5, 12))
    for rel in range(8, 16):
        zs[rel].wait()
    a1 = along_a(1)
    px_relay(0, px0)
    for cp in a0:
        cp.wait()
    b0, over0 = b_start(0)
    for cp in a1:
        cp.wait()
    b1, over1 = b_start(1)
    b_relay(0, b0)
    b_middle(0, b0, over0)
    b_relay(1, b1)
    b_end(0, b0, over0)
    b_middle(1, b1, over1)
    b_end(1, b1, over1)
    px1 = px_start(1, pz1)
    for cp in over0 + over1:
        cp.wait()

    shift = (z + NZ - 4) % NZ
    for k in range(KINDS):
        for s in range(SLOTS):
            for i in range(NX):
                left = jnp.concatenate([L[0, g, s, i, :, k, :] for g in range(2)], 0)
                right = jnp.concatenate([L[1, g, i, s, :, k, :] for g in range(2)], 0)
                rows = pl.ds(k * ALL + s * DP + i * NZ, NZ)
                dproj[rows, :] = pltpu.roll(jnp.concatenate([left, right], 1), shift, 0)
    projs = dproj[...]
    r_norm = lax.rsqrt(jnp.sum(projs * projs, -1, keepdims=True) + epsilon)
    unit = projs * r_norm
    hi, lo = split2(unit)
    u_hi[...] = hi
    u_lo[...] = lo

    def part_of(k):
        rows = pl.ds(k * ALL, ALL)
        return u_hi[rows, :], u_lo[rows, :]

    uq, up, un = part_of(0), part_of(1), part_of(2)
    s_in = score_scale * dot3(uq, up, NTD)
    s_neg = score_scale * dot3(uq, un, NTD)
    lanes = lax.broadcasted_iota(jnp.int32, (ALL, ALL), 1)
    diag = lax.broadcasted_iota(jnp.int32, (ALL, ALL), 0) == lanes
    all_ids = jnp.concatenate(
        [
            pltpu.roll(jnp.concatenate([L[0, g, s, i, :, 3, 0:128] for g in range(2)], 0), shift, 0)
            for s in range(SLOTS)
            for i in range(NX)
        ],
        0,
    ).astype(jnp.int32)
    named = lanes == all_ids[:, 0:1]
    for k in range(1, NEGS):
        named = jnp.logical_or(named, lanes == all_ids[:, k : k + 1])
    ex_in = jnp.exp(s_in)
    ex_neg = jnp.where(named, jnp.exp(s_neg), 0.0)
    total = jnp.sum(ex_in, 1, keepdims=True) + jnp.sum(ex_neg, 1, keepdims=True)
    own_score = jnp.sum(jnp.where(diag, s_in, 0.0), 1, keepdims=True)
    loss_ref[...] = jnp.sum(jnp.log(total) - own_score, 0, keepdims=True) / ALL
    store(loss_ref, loss_hbm)
    factor = (score_scale * loss_scale) / total
    g_in = ex_in * factor - jnp.where(diag, score_scale * loss_scale, 0.0)
    g_neg = ex_neg * factor
    d_uq = dot3(split2(g_in), up) + dot3(split2(g_neg), un)
    d_up = dot3(split2(g_in.T), uq)
    d_un = dot3(split2(g_neg.T), uq)
    d_unit = jnp.concatenate([d_uq, d_up, d_un], 0)
    dproj[...] = (d_unit - unit * jnp.sum(unit * d_unit, -1, keepdims=True)) * r_norm

    px_relay(1, px1)

    own_rows[...] = jnp.zeros_like(own_rows)
    for s in range(SLOTS):
        for k in range(KINDS):
            own_rows[4 * s + k : 4 * s + k + 1, :] = dproj[pl.ds(k * ALL + s * DP + dp, 1), :]
    d_pooled = join3(dot(split3(own_rows[...]), w_ref[...], NTD))
    lifted = d_pooled * gain
    lifted_ref[...] = lifted
    store(lifted_ref, lifted_hbm)
    spread = join3(dot(split3(lifted), xs[...], NTD))
    dot_own[...] = jnp.sum(jnp.where(mine, spread, 0.0), 0, keepdims=True)
    dots_sent = tensor_send(dot_own, dot_land, s_dot, r_dot)

    def line_part(i):
        plains = jnp.concatenate(
            [
                pltpu.roll(jnp.concatenate([PB[g, i, :, k, s, :] for g in range(2)], 0), shift, 0)
                for k in range(KINDS)
                for s in range(SLOTS)
            ],
            0,
        )
        projs = jnp.concatenate(
            [
                dproj[pl.ds(pl.multiple_of(k * ALL + s * DP + i * NZ, NZ), NZ), :]
                for k in range(KINDS)
                for s in range(SLOTS)
            ],
            0,
        )
        parts[i] = dot3(split2(plains), split2(projs), TN)

    for k in (0, 1, 3):
        line_part((x + k) % NX)
    for cp in px0[2:] + px1[2:]:
        cp.wait()
    line_part((x + 2) % NX)
    grad = ((parts[0] + parts[1]) + (parts[2] + parts[3])) / loss_scale
    weighted = grad * w_ref[...].astype(f32)
    fold = weighted[:, 0:128]
    for i in range(1, E // 128):
        fold = fold + weighted[:, i * 128 : (i + 1) * 128]
    gg_ref[...] = exact_dot(jnp.ones((8, 128), f32), fold, NTD)[0:1]
    gw_ref[...] = (grad * gain.T).astype(bf16)
    store(gg_ref, gg_hbm)
    store(gw_ref, gw_hbm)

    dots = tensor_sum(dots_sent, dot_land)

    inner = scales * scales / D * dots
    factors_ref[...] = jnp.concatenate([coeffs, coeffs * inner, jnp.zeros((6, TOK), f32)], 0)
    store(factors_ref, factors_hbm)
    for cp in stores:
        cp.wait()


def finish_kernel(*refs):
    x_hbm, (lifted_hbm, factors_hbm, gw_in, gg_in, loss_in) = refs[0:3], refs[3:8]
    g_hbm, (gw_out, gg_out, loss_out) = refs[8:11], refs[11:14]
    xs, gs, lifted_ref, factors_ref, gw_ref, gg_ref, loss_ref, s_load, s_store = refs[14:]

    def copy(src, dst, sem):
        cp = pltpu.make_async_copy(src, dst, sem)
        cp.start()
        return cp

    def part(ref, i):
        return ref.at[pl.ds(i * SLOTS * LEN, SLOTS * LEN), :]

    first = [copy(factors_hbm, factors_ref, s_load.at[0]), copy(lifted_hbm, lifted_ref, s_load.at[1])]
    states = [copy(x_hbm[i], part(xs, i), s_load.at[2 + i]) for i in range(KINDS)]
    passed = [
        (copy(src, mid, s_load.at[5 + i]), mid, dst)
        for i, (src, mid, dst) in enumerate(
            ((gw_in, gw_ref, gw_out), (gg_in, gg_ref, gg_out), (loss_in, loss_ref, loss_out))
        )
    ]
    for cp in first:
        cp.wait()
    cols = factors_ref[...].T
    stores = []
    for i in range(KINDS):
        states[i].wait()
        for s in range(SLOTS):
            at = (i * SLOTS + s) * LEN
            value = cols[at : at + LEN, 0:1] * lifted_ref[4 * s + i : 4 * s + i + 1, :] - (
                xs[pl.ds(at, LEN), :].astype(f32) * cols[at : at + LEN, 1:2]
            )
            gs[pl.ds(at, LEN), :] = value.astype(bf16)
        stores.append(copy(part(gs, i), g_hbm[i], s_store.at[i]))
        cp, mid, dst = passed[i]
        cp.wait()
        stores.append(copy(mid, dst, s_store.at[KINDS + i]))
    for cp in stores:
        cp.wait()


def body(q, p, n, q_len, p_len, n_len, gain, w, owner, slot):
    hbm = pl.BlockSpec(memory_space=pltpu.HBM)
    dma = pltpu.SemaphoreType.DMA
    states = [v.reshape(SLOTS * LEN, F) for v in (q, p, n)]

    def run(x0, x1, x2, l0, l1, l2, *rest):
        kernel((x0, x1, x2), (l0, l1, l2), *rest)

    state_out = jax.ShapeDtypeStruct((SLOTS * LEN, F), bf16)
    results = pl.pallas_call(
        run,
        out_shape=(
            jax.ShapeDtypeStruct((16, F), f32),
            jax.ShapeDtypeStruct((8, TOK), f32),
            jax.ShapeDtypeStruct((F, E), bf16),
            jax.ShapeDtypeStruct((1, F), f32),
            jax.ShapeDtypeStruct((1, 1), f32),
        ),
        in_specs=[hbm] * 10,
        out_specs=(hbm,) * 5,
        scratch_shapes=[
            pltpu.VMEM((TOK, F), bf16),
            pltpu.VMEM((16, F), f32),
            pltpu.VMEM((8, TOK), f32),
            pltpu.VMEM((F, E), bf16),
            pltpu.VMEM((1, F), f32),
            pltpu.VMEM((1, 1), f32),
            dma((5,)),
            pltpu.SMEM((KINDS, SLOTS), jnp.int32),
            pltpu.VMEM((1, F), f32),
            pltpu.VMEM((F, E), bf16),
            pltpu.VMEM((SLOTS, NEGS), jnp.int32),
            pltpu.VMEM((SLOTS, NEGS), jnp.int32),
            dma((10,)),
            pltpu.VMEM((1, TOK), f32),
            pltpu.VMEM((NT, 1, TOK), f32),
            pltpu.VMEM((1, TOK), f32),
            pltpu.VMEM((NT, 1, TOK), f32),
            pltpu.VMEM((NT, 4, H), f32),
            pltpu.VMEM((NT, 4, H), f32),
            pltpu.VMEM((SLOTS, 1, H), f32),
            pltpu.VMEM((NC, 2, 4, 4, 8, 4, H), f32),
            pltpu.VMEM((2, NX, 8, KINDS, SLOTS, F), f32),
            pltpu.VMEM((SEQ, E), bf16),
            pltpu.VMEM((SEQ, E), bf16),
            pltpu.VMEM((SEQ, E), f32),
            pltpu.VMEM((NX, F, E), f32),
            pltpu.VMEM((16, E), f32),
            dma((NT - 1,)),
            dma((NT - 1,)),
            dma((NT - 1,)),
            dma((NT - 1,)),
            dma((NZ - 1,)),
            dma((NZ - 1,)),
            dma((2, 3)),
            dma((2, 3)),
            dma((2, 6)),
            dma((2, 6)),
            dma((2, 4)),
            dma((2, 4)),
            dma((NT - 1,)),
            dma((NT - 1,)),
            dma((2, 4)),
            dma((2, 4)),
            dma((NZ - 1,)),
            dma((NZ - 1,)),
        ],
        compiler_params=pltpu.CompilerParams(
            collective_id=0, has_side_effects=True, vmem_limit_bytes=62 << 20
        ),
    )(*states, q_len, p_len, n_len, gain.reshape(1, F), w, owner, slot)
    g0, g1, g2, gw, gg, loss = pl.pallas_call(
        finish_kernel,
        out_shape=(state_out,) * 3 + tuple(jax.ShapeDtypeStruct(v.shape, v.dtype) for v in results[2:]),
        in_specs=[hbm] * 8,
        out_specs=(hbm,) * 6,
        scratch_shapes=[
            pltpu.VMEM((TOK, F), bf16),
            pltpu.VMEM((TOK, F), bf16),
            pltpu.VMEM((16, F), f32),
            pltpu.VMEM((8, TOK), f32),
            pltpu.VMEM((F, E), bf16),
            pltpu.VMEM((1, F), f32),
            pltpu.VMEM((1, 1), f32),
            dma((8,)),
            dma((6,)),
        ],
        compiler_params=pltpu.CompilerParams(vmem_limit_bytes=62 << 20),
    )(*states, *results)
    shape = q.shape
    return (
        g0.reshape(shape),
        g1.reshape(shape),
        g2.reshape(shape),
        gw,
        gg.reshape(F),
        loss.reshape(()),
    )


def solution(mesh):
    placed = (
        P("dp", None, "tensor"),
        P("dp", None, "tensor"),
        P("dp", None, "tensor"),
        P("dp"),
        P("dp"),
        P("dp"),
        P("tensor"),
        P("tensor", None),
        P("dp", None),
        P("dp", None),
    )
    return jax.shard_map(
        body,
        mesh=mesh,
        in_specs=placed,
        out_specs=(
            P("dp", None, "tensor"),
            P("dp", None, "tensor"),
            P("dp", None, "tensor"),
            P("tensor", None),
            P("tensor"),
            P(),
        ),
        check_vma=False,
    )
```

```python
import jax
import jax.numpy as jnp
from jax import lax
from jax.experimental import pallas as pl
from jax.experimental.pallas import tpu as pltpu
from jax.sharding import PartitionSpec as P

NX, NY, NZ, NC = 4, 4, 16, 2
NT = NY * NC
DP = NX * NZ
D = 4096
F = D // NT
E = 768
H = E // NC
LEN = 64
SLOTS = 4
NEGS = 7
KINDS = 3
TOK = KINDS * SLOTS * LEN
ALL = SLOTS * DP
SEQ = KINDS * ALL
score_scale = 20.0
loss_scale = 1024.0
epsilon = 1e-06
MESH = pl.DeviceIdType.MESH
f32 = jnp.float32
bf16 = jnp.bfloat16
NN = (((1,), (0,)), ((), ()))
NTD = (((1,), (1,)), ((), ()))
TN = (((0,), (0,)), ((), ()))


def dot(a, b, dims=NN):
    return lax.dot_general(a, b, dims, preferred_element_type=f32)


def exact_dot(a, b, dims=NN):
    return lax.dot_general(a, b, dims, preferred_element_type=f32, precision=lax.Precision.HIGHEST)


def split2(v):
    hi = v.astype(bf16)
    return hi, (v - hi.astype(f32)).astype(bf16)


def split3(v):
    hi = v.astype(bf16)
    rest = v - hi.astype(f32)
    mid = rest.astype(bf16)
    return jnp.concatenate([hi, mid, (rest - mid.astype(f32)).astype(bf16)], 0)


def join3(v):
    return v[0:16] + v[16:32] + v[32:48]


def dot3(a, b, dims=NN):
    return dot(a[0], b[0], dims) + (dot(a[0], b[1], dims) + dot(a[1], b[0], dims))


def kernel(
    x_hbm,
    len_hbm,
    gain_hbm,
    w_hbm,
    owner_hbm,
    slot_hbm,
    lifted_hbm,
    factors_hbm,
    gw_hbm,
    gg_hbm,
    loss_hbm,
    xs,
    lifted_ref,
    factors_ref,
    gw_ref,
    gg_ref,
    loss_ref,
    s_out_copy,
    len_ref,
    gain_ref,
    w_ref,
    owner_ref,
    slot_ref,
    s_in_copy,
    inside,
    sq_own,
    sq_land,
    dot_own,
    dot_land,
    stage,
    rs_land,
    ids_ref,
    L,
    PB,
    u_hi,
    u_lo,
    dproj,
    parts,
    own_rows,
    s_sq,
    r_sq,
    s_rs,
    r_rs,
    s_z,
    r_z,
    s_a,
    r_a,
    s_b,
    r_b,
    s_c,
    r_c,
    s_dot,
    r_dot,
    s_px,
    r_px,
    s_pz,
    r_pz,
):
    dp = lax.axis_index("dp")
    t = lax.axis_index("tensor")
    x, z = dp // NZ, dp % NZ
    y, c = t // NC, t % NC
    a = jnp.where(c == 0, x, y)
    b = jnp.where(c == 0, y, x)

    def tensor_peer(k):
        return (dp, (t + k) % NT)

    def x_peer(k):
        return (((x + k) % NX) * NZ + z, t)

    def y_peer(k):
        return (dp, ((y + k) % NY) * NC + c)

    def z_peer(k):
        return (x * NZ + (z + k) % NZ, t)

    def either(cond, p, q):
        return tuple(jnp.where(cond, i, j) for i, j in zip(p, q))

    def a_peer(k):
        return either(c == 0, x_peer(k), y_peer(k))

    def b_peer(k):
        return either(c == 0, y_peer(k), x_peer(k))

    sibling = (dp, y * NC + 1 - c)

    def send(src, dst, ss, rs, to):
        cp = pltpu.make_async_remote_copy(
            src_ref=src, dst_ref=dst, send_sem=ss, recv_sem=rs, device_id=to, device_id_type=MESH
        )
        cp.start()
        return cp

    loads = []

    def load(src, dst):
        cp = pltpu.make_async_copy(src, dst, s_in_copy.at[len(loads)])
        cp.start()
        loads.append(cp)

    for i in range(KINDS):
        load(x_hbm[i], xs.at[pl.ds(i * SLOTS * LEN, SLOTS * LEN), :])
    for i in range(KINDS):
        load(len_hbm[i], len_ref.at[i])
    load(gain_hbm, gain_ref)
    load(owner_hbm, owner_ref)
    load(slot_hbm, slot_ref)
    load(w_hbm, w_ref)

    stores = []

    def store(src, dst):
        cp = pltpu.make_async_copy(src, dst, s_out_copy.at[len(stores)])
        cp.start()
        stores.append(cp)

    barrier = pltpu.get_barrier_semaphore()
    greeted = (
        [tensor_peer(k) for k in range(1, NT)]
        + [x_peer(k) for k in range(1, NX)]
        + [z_peer(k) for k in (1, 2, NZ - 2, NZ - 1)]
    )
    for peer in greeted:
        pl.semaphore_signal(barrier, inc=1, device_id=peer, device_id_type=MESH)

    ones = jnp.ones((16, 128), bf16)
    for i in range(KINDS):
        loads[i].wait()
        tokens = pl.ds(i * SLOTS * LEN, SLOTS * LEN)
        xf = xs[tokens, :].astype(f32)
        xf = xf * xf
        part = (xf[:, 0:128] + xf[:, 128:256]) + (xf[:, 256:384] + xf[:, 384:512])
        sums = dot(ones, split3(part), NTD)[0:1]
        n = SLOTS * LEN
        sq_own[:, tokens] = (sums[:, 0:n] + sums[:, n : 2 * n]) + sums[:, 2 * n : 3 * n]

    pl.semaphore_wait(barrier, len(greeted))

    def tensor_send(own, land, ss, rs):
        cps = [send(own, land.at[t], ss.at[k - 1], rs.at[k - 1], tensor_peer(k)) for k in range(1, NT)]
        land[t] = own[...]
        return cps

    def tensor_sum(cps, land):
        for cp in cps:
            cp.wait()
        total = land[0]
        for i in range(1, NT):
            total = total + land[i]
        return total

    def greet(i, k):
        for peer in (z_peer(k), z_peer(NZ - k)):
            pl.semaphore_signal(inside.at[i], inc=1, device_id=peer, device_id_type=MESH)

    squares_sent = tensor_send(sq_own, sq_land, s_sq, r_sq)
    greet(0, 2)
    for cp in loads[KINDS:]:
        cp.wait()
    squares = tensor_sum(squares_sent, sq_land)
    pl.semaphore_wait(inside.at[0], 2)
    greet(1, 4)
    scales = lax.rsqrt(squares / D + epsilon)
    lane = lax.broadcasted_iota(jnp.int32, (1, TOK), 1)
    seq = lane // LEN
    lens = jnp.zeros((1, TOK), jnp.int32)
    for i in range(KINDS):
        for s in range(SLOTS):
            lens = jnp.where(seq == i * SLOTS + s, len_ref[i, s], lens)
    live = jnp.where(lane % LEN < lens, 1.0 / lens.astype(f32), 0.0)
    coeffs = scales * live
    row = lax.broadcasted_iota(jnp.int32, (16, TOK), 0)
    mine = (row % 4) * SLOTS + row // 4 == seq
    plain = join3(dot(split3(jnp.where(mine, coeffs, 0.0)), xs[...]))
    for s in range(SLOTS):
        for k in range(KINDS):
            PB[0, x, 4, k, s : s + 1, :] = plain[4 * s + k : 4 * s + k + 1]
    gain = gain_ref[...]
    proj = join3(dot(split3(plain * gain), w_ref[...]))
    for s in range(SLOTS):
        for h in range(NC):
            stage[s * NC + h] = proj[4 * s : 4 * s + 4, h * H : (h + 1) * H]
    cps = [
        send(stage.at[(t + k) % NT], rs_land.at[t], s_rs.at[k - 1], r_rs.at[k - 1], tensor_peer(k))
        for k in range(1, NT)
    ]
    rs_land[t] = stage[t]

    def pz_send(ks):
        block = PB.at[0, x, 4]
        out = []
        for k in ks:
            rel = (4 - k) % NZ
            out.append(send(block, PB.at[rel // 8, x, rel % 8], s_pz.at[k - 1], r_pz.at[k - 1], z_peer(k)))
        return out

    pz0 = pz_send((4, 3, 13, 2, 14, 1, 15))
    ids = (slot_ref[...] * DP + owner_ref[...]).astype(f32)
    ids_ref[...] = jnp.zeros_like(ids_ref)
    for s in range(SLOTS):
        ids_ref[s, :, 0:NEGS] = ids[s : s + 1]
    for cp in cps:
        cp.wait()
    piece = rs_land[0]
    for i in range(1, NT):
        piece = piece + rs_land[i]
    place = lax.broadcasted_iota(jnp.int32, (4, H), 0)
    L[c, 0, b, a, 4] = jnp.where(place == 3, ids_ref[y], piece)
    mine_block = L.at[c, 0, b, a, 4]

    pl.semaphore_wait(inside.at[1], 2)
    zs = {}
    for k in (8, 9, 7, 10, 6, 11, 5, 12, 4, 13, 3, 14, 2, 15, 1):
        rel = (4 - k) % NZ
        zs[rel] = send(mine_block, L.at[c, rel // 8, b, a, rel % 8], s_z.at[k - 1], r_z.at[k - 1], z_peer(k))

    def px_send(g, i, block, k):
        return send(block, block, s_px.at[g, i], r_px.at[g, i], x_peer(k))

    def px_start(g, pz):
        for cp in pz:
            cp.wait()
        return [px_send(g, 0, PB.at[g, x], 1), px_send(g, 1, PB.at[g, x], 3)]

    def px_relay(g, cps):
        cps[0].wait()
        cps.append(px_send(g, 2, PB.at[g, (x + 3) % NX, pl.ds(0, 4)], 1))
        cps[1].wait()
        cps.append(px_send(g, 3, PB.at[g, (x + 1) % NX, pl.ds(4, 4)], 3))

    def along_a(g):
        line = L.at[c, g, b, a]
        return [send(line, line, s_a.at[g, k - 1], r_a.at[g, k - 1], a_peer(k)) for k in (2, 1, 3)]

    def half(g, k, h):
        return L.at[c, g, (b + k) % 4, pl.ds(2 * h, 2)]

    def b_send(g, i, block, k):
        return send(block, block, s_b.at[g, i], r_b.at[g, i], b_peer(k))

    def cross(g, k):
        plane = L.at[c, g, (b + k) % 4]
        return send(plane, plane, s_c.at[g, k], r_c.at[g, k], sibling)

    def b_start(g):
        cps = [
            b_send(g, 0, half(g, 0, 0), 1),
            b_send(g, 1, half(g, 0, 1), 3),
            b_send(g, 2, half(g, 0, 1), 1),
            b_send(g, 3, half(g, 0, 0), 3),
        ]
        return cps, [cross(g, 0)]

    def b_relay(g, cps):
        cps[0].wait()
        cps.append(b_send(g, 4, half(g, 3, 0), 1))
        cps[1].wait()
        cps.append(b_send(g, 5, half(g, 1, 1), 3))

    def b_middle(g, cps, over):
        cps[2].wait()
        over.append(cross(g, 3))
        cps[3].wait()
        over.append(cross(g, 1))

    def b_end(g, cps, over):
        cps[4].wait()
        cps[5].wait()
        over.append(cross(g, 2))

    px0 = px_start(0, pz0)
    for rel in (5, 3, 6, 2, 7, 1, 0):
        zs[rel].wait()
    a0 = along_a(0)
    pz1 = pz_send((8, 9, 7, 10, 6, 11, 5, 12))
    for rel in range(8, 16):
        zs[rel].wait()
    a1 = along_a(1)
    px_relay(0, px0)
    for cp in a0:
        cp.wait()
    b0, over0 = b_start(0)
    for cp in a1:
        cp.wait()
    b1, over1 = b_start(1)
    b_relay(0, b0)
    b_middle(0, b0, over0)
    b_relay(1, b1)
    b_end(0, b0, over0)
    b_middle(1, b1, over1)
    b_end(1, b1, over1)
    px1 = px_start(1, pz1)
    for cp in over0 + over1:
        cp.wait()

    shift = (z + NZ - 4) % NZ
    for k in range(KINDS):
        for s in range(SLOTS):
            for i in range(NX):
                left = jnp.concatenate([L[0, g, s, i, :, k, :] for g in range(2)], 0)
                right = jnp.concatenate([L[1, g, i, s, :, k, :] for g in range(2)], 0)
                rows = pl.ds(k * ALL + s * DP + i * NZ, NZ)
                dproj[rows, :] = pltpu.roll(jnp.concatenate([left, right], 1), shift, 0)
    projs = dproj[...]
    r_norm = lax.rsqrt(jnp.sum(projs * projs, -1, keepdims=True) + epsilon)
    unit = projs * r_norm
    hi, lo = split2(unit)
    u_hi[...] = hi
    u_lo[...] = lo

    def part_of(k):
        rows = pl.ds(k * ALL, ALL)
        return u_hi[rows, :], u_lo[rows, :]

    uq, up, un = part_of(0), part_of(1), part_of(2)
    s_in = score_scale * dot3(uq, up, NTD)
    s_neg = score_scale * dot3(uq, un, NTD)
    lanes = lax.broadcasted_iota(jnp.int32, (ALL, ALL), 1)
    diag = lax.broadcasted_iota(jnp.int32, (ALL, ALL), 0) == lanes
    all_ids = jnp.concatenate(
        [
            pltpu.roll(jnp.concatenate([L[0, g, s, i, :, 3, 0:128] for g in range(2)], 0), shift, 0)
            for s in range(SLOTS)
            for i in range(NX)
        ],
        0,
    ).astype(jnp.int32)
    named = lanes == all_ids[:, 0:1]
    for k in range(1, NEGS):
        named = jnp.logical_or(named, lanes == all_ids[:, k : k + 1])
    ex_in = jnp.exp(s_in)
    ex_neg = jnp.where(named, jnp.exp(s_neg), 0.0)
    total = jnp.sum(ex_in, 1, keepdims=True) + jnp.sum(ex_neg, 1, keepdims=True)
    own_score = jnp.sum(jnp.where(diag, s_in, 0.0), 1, keepdims=True)
    loss_ref[...] = jnp.sum(jnp.log(total) - own_score, 0, keepdims=True) / ALL
    store(loss_ref, loss_hbm)
    factor = (score_scale * loss_scale) / total
    g_in = ex_in * factor - jnp.where(diag, score_scale * loss_scale, 0.0)
    g_neg = ex_neg * factor
    d_uq = dot3(split2(g_in), up) + dot3(split2(g_neg), un)
    d_up = dot3(split2(g_in.T), uq)
    d_un = dot3(split2(g_neg.T), uq)
    d_unit = jnp.concatenate([d_uq, d_up, d_un], 0)
    dproj[...] = (d_unit - unit * jnp.sum(unit * d_unit, -1, keepdims=True)) * r_norm

    px_relay(1, px1)

    own_rows[...] = jnp.zeros_like(own_rows)
    for s in range(SLOTS):
        for k in range(KINDS):
            own_rows[4 * s + k : 4 * s + k + 1, :] = dproj[pl.ds(k * ALL + s * DP + dp, 1), :]
    d_pooled = join3(dot(split3(own_rows[...]), w_ref[...], NTD))
    lifted = d_pooled * gain
    lifted_ref[...] = lifted
    store(lifted_ref, lifted_hbm)
    spread = join3(dot(split3(lifted), xs[...], NTD))
    dot_own[...] = jnp.sum(jnp.where(mine, spread, 0.0), 0, keepdims=True)
    dots_sent = tensor_send(dot_own, dot_land, s_dot, r_dot)

    def line_part(i):
        plains = jnp.concatenate(
            [
                pltpu.roll(jnp.concatenate([PB[g, i, :, k, s, :] for g in range(2)], 0), shift, 0)
                for k in range(KINDS)
                for s in range(SLOTS)
            ],
            0,
        )
        projs = jnp.concatenate(
            [
                dproj[pl.ds(pl.multiple_of(k * ALL + s * DP + i * NZ, NZ), NZ), :]
                for k in range(KINDS)
                for s in range(SLOTS)
            ],
            0,
        )
        parts[i] = dot3(split2(plains), split2(projs), TN)

    for k in (0, 1, 3):
        line_part((x + k) % NX)
    for cp in px0[2:] + px1[2:]:
        cp.wait()
    line_part((x + 2) % NX)
    grad = ((parts[0] + parts[1]) + (parts[2] + parts[3])) / loss_scale
    weighted = grad * w_ref[...].astype(f32)
    fold = weighted[:, 0:128]
    for i in range(1, E // 128):
        fold = fold + weighted[:, i * 128 : (i + 1) * 128]
    gg_ref[...] = exact_dot(jnp.ones((8, 128), f32), fold, NTD)[0:1]
    gw_ref[...] = (grad * gain.T).astype(bf16)
    store(gg_ref, gg_hbm)
    store(gw_ref, gw_hbm)

    dots = tensor_sum(dots_sent, dot_land)

    inner = scales * scales / D * dots
    factors_ref[...] = jnp.concatenate([coeffs, coeffs * inner, jnp.zeros((6, TOK), f32)], 0)
    store(factors_ref, factors_hbm)
    for cp in stores:
        cp.wait()


def finish_kernel(*refs):
    x_hbm, (lifted_hbm, factors_hbm, gw_in, gg_in, loss_in) = refs[0:3], refs[3:8]
    g_hbm, (gw_out, gg_out, loss_out) = refs[8:11], refs[11:14]
    xs, gs, lifted_ref, factors_ref, gw_ref, gg_ref, loss_ref, s_load, s_store = refs[14:]

    def copy(src, dst, sem):
        cp = pltpu.make_async_copy(src, dst, sem)
        cp.start()
        return cp

    def part(ref, i):
        return ref.at[pl.ds(i * SLOTS * LEN, SLOTS * LEN), :]

    first = [copy(factors_hbm, factors_ref, s_load.at[0]), copy(lifted_hbm, lifted_ref, s_load.at[1])]
    states = [copy(x_hbm[i], part(xs, i), s_load.at[2 + i]) for i in range(KINDS)]
    passed = [
        (copy(src, mid, s_load.at[5 + i]), mid, dst)
        for i, (src, mid, dst) in enumerate(
            ((gw_in, gw_ref, gw_out), (gg_in, gg_ref, gg_out), (loss_in, loss_ref, loss_out))
        )
    ]
    for cp in first:
        cp.wait()
    cols = factors_ref[...].T
    stores = []
    for i in range(KINDS):
        states[i].wait()
        for s in range(SLOTS):
            at = (i * SLOTS + s) * LEN
            value = cols[at : at + LEN, 0:1] * lifted_ref[4 * s + i : 4 * s + i + 1, :] - (
                xs[pl.ds(at, LEN), :].astype(f32) * cols[at : at + LEN, 1:2]
            )
            gs[pl.ds(at, LEN), :] = value.astype(bf16)
        stores.append(copy(part(gs, i), g_hbm[i], s_store.at[i]))
        cp, mid, dst = passed[i]
        cp.wait()
        stores.append(copy(mid, dst, s_store.at[KINDS + i]))
    for cp in stores:
        cp.wait()


def body(q, p, n, q_len, p_len, n_len, gain, w, owner, slot):
    hbm = pl.BlockSpec(memory_space=pltpu.HBM)
    dma = pltpu.SemaphoreType.DMA
    states = [v.reshape(SLOTS * LEN, F) for v in (q, p, n)]

    def run(x0, x1, x2, l0, l1, l2, *rest):
        kernel((x0, x1, x2), (l0, l1, l2), *rest)

    state_out = jax.ShapeDtypeStruct((SLOTS * LEN, F), bf16)
    results = pl.pallas_call(
        run,
        out_shape=(
            jax.ShapeDtypeStruct((16, F), f32),
            jax.ShapeDtypeStruct((8, TOK), f32),
            jax.ShapeDtypeStruct((F, E), bf16),
            jax.ShapeDtypeStruct((1, F), f32),
            jax.ShapeDtypeStruct((1, 1), f32),
        ),
        in_specs=[hbm] * 10,
        out_specs=(hbm,) * 5,
        scratch_shapes=[
            pltpu.VMEM((TOK, F), bf16),
            pltpu.VMEM((16, F), f32),
            pltpu.VMEM((8, TOK), f32),
            pltpu.VMEM((F, E), bf16),
            pltpu.VMEM((1, F), f32),
            pltpu.VMEM((1, 1), f32),
            dma((5,)),
            pltpu.SMEM((KINDS, SLOTS), jnp.int32),
            pltpu.VMEM((1, F), f32),
            pltpu.VMEM((F, E), bf16),
            pltpu.VMEM((SLOTS, NEGS), jnp.int32),
            pltpu.VMEM((SLOTS, NEGS), jnp.int32),
            dma((10,)),
            pltpu.SemaphoreType.REGULAR((2,)),
            pltpu.VMEM((1, TOK), f32),
            pltpu.VMEM((NT, 1, TOK), f32),
            pltpu.VMEM((1, TOK), f32),
            pltpu.VMEM((NT, 1, TOK), f32),
            pltpu.VMEM((NT, 4, H), f32),
            pltpu.VMEM((NT, 4, H), f32),
            pltpu.VMEM((SLOTS, 1, H), f32),
            pltpu.VMEM((NC, 2, 4, 4, 8, 4, H), f32),
            pltpu.VMEM((2, NX, 8, KINDS, SLOTS, F), f32),
            pltpu.VMEM((SEQ, E), bf16),
            pltpu.VMEM((SEQ, E), bf16),
            pltpu.VMEM((SEQ, E), f32),
            pltpu.VMEM((NX, F, E), f32),
            pltpu.VMEM((16, E), f32),
            dma((NT - 1,)),
            dma((NT - 1,)),
            dma((NT - 1,)),
            dma((NT - 1,)),
            dma((NZ - 1,)),
            dma((NZ - 1,)),
            dma((2, 3)),
            dma((2, 3)),
            dma((2, 6)),
            dma((2, 6)),
            dma((2, 4)),
            dma((2, 4)),
            dma((NT - 1,)),
            dma((NT - 1,)),
            dma((2, 4)),
            dma((2, 4)),
            dma((NZ - 1,)),
            dma((NZ - 1,)),
        ],
        compiler_params=pltpu.CompilerParams(
            collective_id=0, has_side_effects=True, vmem_limit_bytes=62 << 20
        ),
    )(*states, q_len, p_len, n_len, gain.reshape(1, F), w, owner, slot)
    g0, g1, g2, gw, gg, loss = pl.pallas_call(
        finish_kernel,
        out_shape=(state_out,) * 3 + tuple(jax.ShapeDtypeStruct(v.shape, v.dtype) for v in results[2:]),
        in_specs=[hbm] * 8,
        out_specs=(hbm,) * 6,
        scratch_shapes=[
            pltpu.VMEM((TOK, F), bf16),
            pltpu.VMEM((TOK, F), bf16),
            pltpu.VMEM((16, F), f32),
            pltpu.VMEM((8, TOK), f32),
            pltpu.VMEM((F, E), bf16),
            pltpu.VMEM((1, F), f32),
            pltpu.VMEM((1, 1), f32),
            dma((8,)),
            dma((6,)),
        ],
        compiler_params=pltpu.CompilerParams(vmem_limit_bytes=62 << 20),
    )(*states, *results)
    shape = q.shape
    return (
        g0.reshape(shape),
        g1.reshape(shape),
        g2.reshape(shape),
        gw,
        gg.reshape(F),
        loss.reshape(()),
    )


def solution(mesh):
    placed = (
        P("dp", None, "tensor"),
        P("dp", None, "tensor"),
        P("dp", None, "tensor"),
        P("dp"),
        P("dp"),
        P("dp"),
        P("tensor"),
        P("tensor", None),
        P("dp", None),
        P("dp", None),
    )
    return jax.shard_map(
        body,
        mesh=mesh,
        in_specs=placed,
        out_specs=(
            P("dp", None, "tensor"),
            P("dp", None, "tensor"),
            P("dp", None, "tensor"),
            P("tensor", None),
            P("tensor"),
            P(),
        ),
        check_vma=False,
    )
```

```python
import jax
import jax.numpy as jnp
from jax import lax
from jax.experimental import pallas as pl
from jax.experimental.pallas import tpu as pltpu
from jax.sharding import PartitionSpec as P

NX, NY, NZ, NC = 4, 4, 16, 2
NT = NY * NC
DP = NX * NZ
D = 4096
F = D // NT
E = 768
H = E // NC
LEN = 64
SLOTS = 4
NEGS = 7
KINDS = 3
TOK = KINDS * SLOTS * LEN
ALL = SLOTS * DP
SEQ = KINDS * ALL
score_scale = 20.0
loss_scale = 1024.0
epsilon = 1e-06
MESH = pl.DeviceIdType.MESH
f32 = jnp.float32
bf16 = jnp.bfloat16
NN = (((1,), (0,)), ((), ()))
NTD = (((1,), (1,)), ((), ()))
TN = (((0,), (0,)), ((), ()))


def dot(a, b, dims=NN):
    return lax.dot_general(a, b, dims, preferred_element_type=f32)


def exact_dot(a, b, dims=NN):
    return lax.dot_general(a, b, dims, preferred_element_type=f32, precision=lax.Precision.HIGHEST)


def split2(v):
    hi = v.astype(bf16)
    return hi, (v - hi.astype(f32)).astype(bf16)


def split3(v):
    hi = v.astype(bf16)
    rest = v - hi.astype(f32)
    mid = rest.astype(bf16)
    return jnp.concatenate([hi, mid, (rest - mid.astype(f32)).astype(bf16)], 0)


def join3(v):
    return v[0:16] + v[16:32] + v[32:48]


def dot3(a, b, dims=NN):
    return dot(a[0], b[0], dims) + (dot(a[0], b[1], dims) + dot(a[1], b[0], dims))


def kernel(
    x_hbm,
    len_hbm,
    gain_hbm,
    w_hbm,
    owner_hbm,
    slot_hbm,
    lifted_hbm,
    factors_hbm,
    gw_hbm,
    gg_hbm,
    loss_hbm,
    xs,
    lifted_ref,
    factors_ref,
    gw_ref,
    gg_ref,
    loss_ref,
    s_out_copy,
    len_ref,
    gain_ref,
    w_ref,
    owner_ref,
    slot_ref,
    s_in_copy,
    inside,
    sq_own,
    sq_land,
    dot_own,
    dot_land,
    stage,
    rs_land,
    ids_ref,
    L,
    PB,
    u_hi,
    u_lo,
    dproj,
    parts,
    own_rows,
    s_sq,
    r_sq,
    s_rs,
    r_rs,
    s_z,
    r_z,
    s_a,
    r_a,
    s_b,
    r_b,
    s_c,
    r_c,
    s_dot,
    r_dot,
    s_px,
    r_px,
    s_pz,
    r_pz,
):
    dp = lax.axis_index("dp")
    t = lax.axis_index("tensor")
    x, z = dp // NZ, dp % NZ
    y, c = t // NC, t % NC
    a = jnp.where(c == 0, x, y)
    b = jnp.where(c == 0, y, x)

    def tensor_peer(k):
        return (dp, (t + k) % NT)

    def x_peer(k):
        return (((x + k) % NX) * NZ + z, t)

    def y_peer(k):
        return (dp, ((y + k) % NY) * NC + c)

    def z_peer(k):
        return (x * NZ + (z + k) % NZ, t)

    def either(cond, p, q):
        return tuple(jnp.where(cond, i, j) for i, j in zip(p, q))

    def a_peer(k):
        return either(c == 0, x_peer(k), y_peer(k))

    def b_peer(k):
        return either(c == 0, y_peer(k), x_peer(k))

    sibling = (dp, y * NC + 1 - c)

    def send(src, dst, ss, rs, to):
        cp = pltpu.make_async_remote_copy(
            src_ref=src, dst_ref=dst, send_sem=ss, recv_sem=rs, device_id=to, device_id_type=MESH
        )
        cp.start()
        return cp

    loads = []

    def load(src, dst):
        cp = pltpu.make_async_copy(src, dst, s_in_copy.at[len(loads)])
        cp.start()
        loads.append(cp)

    for i in range(KINDS):
        load(x_hbm[i], xs.at[pl.ds(i * SLOTS * LEN, SLOTS * LEN), :])
    for i in range(KINDS):
        load(len_hbm[i], len_ref.at[i])
    load(gain_hbm, gain_ref)
    load(owner_hbm, owner_ref)
    load(slot_hbm, slot_ref)
    load(w_hbm, w_ref)

    stores = []

    def store(src, dst):
        cp = pltpu.make_async_copy(src, dst, s_out_copy.at[len(stores)])
        cp.start()
        stores.append(cp)

    barrier = pltpu.get_barrier_semaphore()
    greeted = (
        [tensor_peer(k) for k in range(1, NT)]
        + [x_peer(k) for k in range(1, NX)]
        + [z_peer(k) for k in (1, 2, NZ - 2, NZ - 1)]
    )
    for peer in greeted:
        pl.semaphore_signal(barrier, inc=1, device_id=peer, device_id_type=MESH)

    ones = jnp.ones((16, 128), bf16)
    for i in range(KINDS):
        loads[i].wait()
        tokens = pl.ds(i * SLOTS * LEN, SLOTS * LEN)
        xf = xs[tokens, :].astype(f32)
        xf = xf * xf
        part = (xf[:, 0:128] + xf[:, 128:256]) + (xf[:, 256:384] + xf[:, 384:512])
        sums = dot(ones, split3(part), NTD)[0:1]
        n = SLOTS * LEN
        sq_own[:, tokens] = (sums[:, 0:n] + sums[:, n : 2 * n]) + sums[:, 2 * n : 3 * n]

    pl.semaphore_wait(barrier, len(greeted))

    def tensor_send(own, land, ss, rs):
        cps = [send(own, land.at[t], ss.at[k - 1], rs.at[k - 1], tensor_peer(k)) for k in range(1, NT)]
        land[t] = own[...]
        return cps

    def tensor_sum(cps, land):
        for cp in cps:
            cp.wait()
        total = land[0]
        for i in range(1, NT):
            total = total + land[i]
        return total

    def greet(i, k):
        for peer in (z_peer(k), z_peer(NZ - k)):
            pl.semaphore_signal(inside.at[i], inc=1, device_id=peer, device_id_type=MESH)

    squares_sent = tensor_send(sq_own, sq_land, s_sq, r_sq)
    greet(0, 2)
    for cp in loads[KINDS:]:
        cp.wait()
    squares = tensor_sum(squares_sent, sq_land)
    pl.semaphore_wait(inside.at[0], 2)
    greet(1, 4)
    scales = lax.rsqrt(squares / D + epsilon)
    lane = lax.broadcasted_iota(jnp.int32, (1, TOK), 1)
    seq = lane // LEN
    lens = jnp.zeros((1, TOK), jnp.int32)
    for i in range(KINDS):
        for s in range(SLOTS):
            lens = jnp.where(seq == i * SLOTS + s, len_ref[i, s], lens)
    live = jnp.where(lane % LEN < lens, 1.0 / lens.astype(f32), 0.0)
    coeffs = scales * live
    row = lax.broadcasted_iota(jnp.int32, (16, TOK), 0)
    mine = (row % 4) * SLOTS + row // 4 == seq
    plain = join3(dot(split3(jnp.where(mine, coeffs, 0.0)), xs[...]))
    for s in range(SLOTS):
        for k in range(KINDS):
            PB[0, x, 4, k, s : s + 1, :] = plain[4 * s + k : 4 * s + k + 1]
    gain = gain_ref[...]
    proj = join3(dot(split3(plain * gain), w_ref[...]))
    for s in range(SLOTS):
        for h in range(NC):
            stage[s * NC + h] = proj[4 * s : 4 * s + 4, h * H : (h + 1) * H]
    cps = [
        send(stage.at[(t + k) % NT], rs_land.at[t], s_rs.at[k - 1], r_rs.at[k - 1], tensor_peer(k))
        for k in range(1, NT)
    ]
    rs_land[t] = stage[t]

    def pz_send(ks):
        block = PB.at[0, x, 4]
        out = []
        for k in ks:
            rel = (4 - k) % NZ
            out.append(send(block, PB.at[rel // 8, x, rel % 8], s_pz.at[k - 1], r_pz.at[k - 1], z_peer(k)))
        return out

    pz0 = pz_send((4, 3, 13, 2, 14, 1, 15))
    ids = (slot_ref[...] * DP + owner_ref[...]).astype(f32)
    ids_ref[...] = jnp.zeros_like(ids_ref)
    for s in range(SLOTS):
        ids_ref[s, :, 0:NEGS] = ids[s : s + 1]
    for cp in cps:
        cp.wait()
    piece = rs_land[0]
    for i in range(1, NT):
        piece = piece + rs_land[i]
    place = lax.broadcasted_iota(jnp.int32, (4, H), 0)
    L[c, 0, b, a, 4] = jnp.where(place == 3, ids_ref[y], piece)
    mine_block = L.at[c, 0, b, a, 4]

    pl.semaphore_wait(inside.at[1], 2)
    zs = {}
    for k in (8, 9, 7, 10, 6, 11, 5, 12, 4, 13, 3, 14, 2, 15, 1):
        rel = (4 - k) % NZ
        zs[rel] = send(mine_block, L.at[c, rel // 8, b, a, rel % 8], s_z.at[k - 1], r_z.at[k - 1], z_peer(k))

    def px_send(g, i, block, k):
        return send(block, block, s_px.at[g, i], r_px.at[g, i], x_peer(k))

    def px_start(g, pz):
        for cp in pz:
            cp.wait()
        return [px_send(g, 0, PB.at[g, x], 1), px_send(g, 1, PB.at[g, x], 3)]

    def px_relay(g, cps):
        cps[0].wait()
        cps.append(px_send(g, 2, PB.at[g, (x + 3) % NX, pl.ds(0, 4)], 1))
        cps[1].wait()
        cps.append(px_send(g, 3, PB.at[g, (x + 1) % NX, pl.ds(4, 4)], 3))

    def along_a(g):
        line = L.at[c, g, b, a]
        return [send(line, line, s_a.at[g, k - 1], r_a.at[g, k - 1], a_peer(k)) for k in (2, 1, 3)]

    def half(g, k, h):
        return L.at[c, g, (b + k) % 4, pl.ds(2 * h, 2)]

    def b_send(g, i, block, k):
        return send(block, block, s_b.at[g, i], r_b.at[g, i], b_peer(k))

    def cross(g, k):
        plane = L.at[c, g, (b + k) % 4]
        return send(plane, plane, s_c.at[g, k], r_c.at[g, k], sibling)

    def b_start(g):
        cps = [
            b_send(g, 0, half(g, 0, 0), 1),
            b_send(g, 1, half(g, 0, 1), 3),
            b_send(g, 2, half(g, 0, 1), 1),
            b_send(g, 3, half(g, 0, 0), 3),
        ]
        return cps, [cross(g, 0)]

    def b_relay(g, cps):
        cps[0].wait()
        cps.append(b_send(g, 4, half(g, 3, 0), 1))
        cps[1].wait()
        cps.append(b_send(g, 5, half(g, 1, 1), 3))

    def b_middle(g, cps, over):
        cps[2].wait()
        over.append(cross(g, 3))
        cps[3].wait()
        over.append(cross(g, 1))

    def b_end(g, cps, over):
        cps[4].wait()
        cps[5].wait()
        over.append(cross(g, 2))

    px0 = px_start(0, pz0)
    for rel in (5, 3, 6, 2, 7, 1, 0):
        zs[rel].wait()
    a0 = along_a(0)
    pz1 = pz_send((8, 9, 7, 10, 6, 11, 5, 12))
    for rel in range(8, 16):
        zs[rel].wait()
    a1 = along_a(1)
    px_relay(0, px0)
    for cp in a0:
        cp.wait()
    b0, over0 = b_start(0)
    for cp in a1:
        cp.wait()
    b1, over1 = b_start(1)
    b_relay(0, b0)
    b_middle(0, b0, over0)
    b_relay(1, b1)
    b_end(0, b0, over0)
    b_middle(1, b1, over1)
    b_end(1, b1, over1)
    px1 = px_start(1, pz1)
    for cp in over0 + over1:
        cp.wait()

    shift = (z + NZ - 4) % NZ
    for k in range(KINDS):
        for s in range(SLOTS):
            for i in range(NX):
                left = jnp.concatenate([L[0, g, s, i, :, k, :] for g in range(2)], 0)
                right = jnp.concatenate([L[1, g, i, s, :, k, :] for g in range(2)], 0)
                rows = pl.ds(k * ALL + s * DP + i * NZ, NZ)
                dproj[rows, :] = pltpu.roll(jnp.concatenate([left, right], 1), shift, 0)
    projs = dproj[...]
    r_norm = lax.rsqrt(jnp.sum(projs * projs, -1, keepdims=True) + epsilon)
    unit = projs * r_norm
    hi, lo = split2(unit)
    u_hi[...] = hi
    u_lo[...] = lo

    def part_of(k):
        rows = pl.ds(k * ALL, ALL)
        return u_hi[rows, :], u_lo[rows, :]

    uq, up, un = part_of(0), part_of(1), part_of(2)
    s_in = score_scale * dot3(uq, up, NTD)
    s_neg = score_scale * dot3(uq, un, NTD)
    lanes = lax.broadcasted_iota(jnp.int32, (ALL, ALL), 1)
    diag = lax.broadcasted_iota(jnp.int32, (ALL, ALL), 0) == lanes
    all_ids = jnp.concatenate(
        [
            pltpu.roll(jnp.concatenate([L[0, g, s, i, :, 3, 0:128] for g in range(2)], 0), shift, 0)
            for s in range(SLOTS)
            for i in range(NX)
        ],
        0,
    ).astype(jnp.int32)
    named = lanes == all_ids[:, 0:1]
    for k in range(1, NEGS):
        named = jnp.logical_or(named, lanes == all_ids[:, k : k + 1])
    ex_in = jnp.exp(s_in)
    ex_neg = jnp.where(named, jnp.exp(s_neg), 0.0)
    total = jnp.sum(ex_in, 1, keepdims=True) + jnp.sum(ex_neg, 1, keepdims=True)
    own_score = jnp.sum(jnp.where(diag, s_in, 0.0), 1, keepdims=True)
    loss_ref[...] = jnp.sum(jnp.log(total) - own_score, 0, keepdims=True) / ALL
    store(loss_ref, loss_hbm)
    factor = (score_scale * loss_scale) / total
    g_in = ex_in * factor - jnp.where(diag, score_scale * loss_scale, 0.0)
    g_neg = ex_neg * factor
    d_uq = dot3(split2(g_in), up) + dot3(split2(g_neg), un)
    d_up = dot3(split2(g_in.T), uq)
    d_un = dot3(split2(g_neg.T), uq)
    d_unit = jnp.concatenate([d_uq, d_up, d_un], 0)
    at_in = g_in * s_in
    at_neg = g_neg * s_neg
    columns = jnp.concatenate(
        [jnp.sum(at_in, 0, keepdims=True), jnp.sum(at_neg, 0, keepdims=True), jnp.zeros((6, ALL), f32)], 0
    ).T
    along = jnp.concatenate(
        [jnp.sum(at_in + at_neg, 1, keepdims=True), columns[:, 0:1], columns[:, 1:2]], 0
    ) / score_scale
    dproj[...] = (d_unit - unit * along) * r_norm

    px_relay(1, px1)

    own_rows[...] = jnp.zeros_like(own_rows)
    for s in range(SLOTS):
        for k in range(KINDS):
            own_rows[4 * s + k : 4 * s + k + 1, :] = dproj[pl.ds(k * ALL + s * DP + dp, 1), :]
    d_pooled = join3(dot(split3(own_rows[...]), w_ref[...], NTD))
    lifted = d_pooled * gain
    lifted_ref[...] = lifted
    store(lifted_ref, lifted_hbm)
    spread = join3(dot(split3(lifted), xs[...], NTD))
    dot_own[...] = jnp.sum(jnp.where(mine, spread, 0.0), 0, keepdims=True)
    dots_sent = tensor_send(dot_own, dot_land, s_dot, r_dot)

    def line_part(i):
        plains = jnp.concatenate(
            [
                pltpu.roll(jnp.concatenate([PB[g, i, :, k, s, :] for g in range(2)], 0), shift, 0)
                for k in range(KINDS)
                for s in range(SLOTS)
            ],
            0,
        )
        projs = jnp.concatenate(
            [
                dproj[pl.ds(pl.multiple_of(k * ALL + s * DP + i * NZ, NZ), NZ), :]
                for k in range(KINDS)
                for s in range(SLOTS)
            ],
            0,
        )
        return dot3(split2(plains), split2(projs), TN)

    parts[0] = line_part(x)
    parts[1] = line_part((x + 1) % NX)
    parts[1] = parts[1] + line_part((x + 3) % NX)
    for cp in px0[2:] + px1[2:]:
        cp.wait()
    grad = ((parts[0] + line_part((x + 2) % NX)) + parts[1]) / loss_scale
    weighted = grad * w_ref[...].astype(f32)
    fold = weighted[:, 0:128]
    for i in range(1, E // 128):
        fold = fold + weighted[:, i * 128 : (i + 1) * 128]
    gg_ref[...] = exact_dot(jnp.ones((8, 128), f32), fold, NTD)[0:1]
    gw_ref[...] = (grad * gain.T).astype(bf16)
    store(gg_ref, gg_hbm)
    store(gw_ref, gw_hbm)

    dots = tensor_sum(dots_sent, dot_land)

    inner = scales * scales / D * dots
    factors_ref[...] = jnp.concatenate([coeffs, coeffs * inner, jnp.zeros((6, TOK), f32)], 0)
    store(factors_ref, factors_hbm)
    for cp in stores:
        cp.wait()


def finish_kernel(*refs):
    x_hbm, (lifted_hbm, factors_hbm, gw_in, gg_in, loss_in) = refs[0:3], refs[3:8]
    g_hbm, (gw_out, gg_out, loss_out) = refs[8:11], refs[11:14]
    xs, gs, lifted_ref, factors_ref, gw_ref, gg_ref, loss_ref, s_load, s_store = refs[14:]

    def copy(src, dst, sem):
        cp = pltpu.make_async_copy(src, dst, sem)
        cp.start()
        return cp

    def part(ref, i):
        return ref.at[pl.ds(i * SLOTS * LEN, SLOTS * LEN), :]

    first = [copy(factors_hbm, factors_ref, s_load.at[0]), copy(lifted_hbm, lifted_ref, s_load.at[1])]
    states = [copy(x_hbm[i], part(xs, i), s_load.at[2 + i]) for i in range(KINDS)]
    passed = [
        (copy(src, mid, s_load.at[5 + i]), mid, dst)
        for i, (src, mid, dst) in enumerate(
            ((gw_in, gw_ref, gw_out), (gg_in, gg_ref, gg_out), (loss_in, loss_ref, loss_out))
        )
    ]
    for cp in first:
        cp.wait()
    cols = factors_ref[...].T
    stores = []
    for i in range(KINDS):
        states[i].wait()
        for s in range(SLOTS):
            at = (i * SLOTS + s) * LEN
            value = cols[at : at + LEN, 0:1] * lifted_ref[4 * s + i : 4 * s + i + 1, :] - (
                xs[pl.ds(at, LEN), :].astype(f32) * cols[at : at + LEN, 1:2]
            )
            gs[pl.ds(at, LEN), :] = value.astype(bf16)
        stores.append(copy(part(gs, i), g_hbm[i], s_store.at[i]))
        cp, mid, dst = passed[i]
        cp.wait()
        stores.append(copy(mid, dst, s_store.at[KINDS + i]))
    for cp in stores:
        cp.wait()


def body(q, p, n, q_len, p_len, n_len, gain, w, owner, slot):
    hbm = pl.BlockSpec(memory_space=pltpu.HBM)
    dma = pltpu.SemaphoreType.DMA
    states = [v.reshape(SLOTS * LEN, F) for v in (q, p, n)]

    def run(x0, x1, x2, l0, l1, l2, *rest):
        kernel((x0, x1, x2), (l0, l1, l2), *rest)

    state_out = jax.ShapeDtypeStruct((SLOTS * LEN, F), bf16)
    results = pl.pallas_call(
        run,
        out_shape=(
            jax.ShapeDtypeStruct((16, F), f32),
            jax.ShapeDtypeStruct((8, TOK), f32),
            jax.ShapeDtypeStruct((F, E), bf16),
            jax.ShapeDtypeStruct((1, F), f32),
            jax.ShapeDtypeStruct((1, 1), f32),
        ),
        in_specs=[hbm] * 10,
        out_specs=(hbm,) * 5,
        scratch_shapes=[
            pltpu.VMEM((TOK, F), bf16),
            pltpu.VMEM((16, F), f32),
            pltpu.VMEM((8, TOK), f32),
            pltpu.VMEM((F, E), bf16),
            pltpu.VMEM((1, F), f32),
            pltpu.VMEM((1, 1), f32),
            dma((5,)),
            pltpu.SMEM((KINDS, SLOTS), jnp.int32),
            pltpu.VMEM((1, F), f32),
            pltpu.VMEM((F, E), bf16),
            pltpu.VMEM((SLOTS, NEGS), jnp.int32),
            pltpu.VMEM((SLOTS, NEGS), jnp.int32),
            dma((10,)),
            pltpu.SemaphoreType.REGULAR((2,)),
            pltpu.VMEM((1, TOK), f32),
            pltpu.VMEM((NT, 1, TOK), f32),
            pltpu.VMEM((1, TOK), f32),
            pltpu.VMEM((NT, 1, TOK), f32),
            pltpu.VMEM((NT, 4, H), f32),
            pltpu.VMEM((NT, 4, H), f32),
            pltpu.VMEM((SLOTS, 1, H), f32),
            pltpu.VMEM((NC, 2, 4, 4, 8, 4, H), f32),
            pltpu.VMEM((2, NX, 8, KINDS, SLOTS, F), f32),
            pltpu.VMEM((SEQ, E), bf16),
            pltpu.VMEM((SEQ, E), bf16),
            pltpu.VMEM((SEQ, E), f32),
            pltpu.VMEM((2, F, E), f32),
            pltpu.VMEM((16, E), f32),
            dma((NT - 1,)),
            dma((NT - 1,)),
            dma((NT - 1,)),
            dma((NT - 1,)),
            dma((NZ - 1,)),
            dma((NZ - 1,)),
            dma((2, 3)),
            dma((2, 3)),
            dma((2, 6)),
            dma((2, 6)),
            dma((2, 4)),
            dma((2, 4)),
            dma((NT - 1,)),
            dma((NT - 1,)),
            dma((2, 4)),
            dma((2, 4)),
            dma((NZ - 1,)),
            dma((NZ - 1,)),
        ],
        compiler_params=pltpu.CompilerParams(
            collective_id=0, has_side_effects=True, vmem_limit_bytes=62 << 20
        ),
    )(*states, q_len, p_len, n_len, gain.reshape(1, F), w, owner, slot)
    g0, g1, g2, gw, gg, loss = pl.pallas_call(
        finish_kernel,
        out_shape=(state_out,) * 3 + tuple(jax.ShapeDtypeStruct(v.shape, v.dtype) for v in results[2:]),
        in_specs=[hbm] * 8,
        out_specs=(hbm,) * 6,
        scratch_shapes=[
            pltpu.VMEM((TOK, F), bf16),
            pltpu.VMEM((TOK, F), bf16),
            pltpu.VMEM((16, F), f32),
            pltpu.VMEM((8, TOK), f32),
            pltpu.VMEM((F, E), bf16),
            pltpu.VMEM((1, F), f32),
            pltpu.VMEM((1, 1), f32),
            dma((8,)),
            dma((6,)),
        ],
        compiler_params=pltpu.CompilerParams(vmem_limit_bytes=62 << 20),
    )(*states, *results)
    shape = q.shape
    return (
        g0.reshape(shape),
        g1.reshape(shape),
        g2.reshape(shape),
        gw,
        gg.reshape(F),
        loss.reshape(()),
    )


def solution(mesh):
    placed = (
        P("dp", None, "tensor"),
        P("dp", None, "tensor"),
        P("dp", None, "tensor"),
        P("dp"),
        P("dp"),
        P("dp"),
        P("tensor"),
        P("tensor", None),
        P("dp", None),
        P("dp", None),
    )
    return jax.shard_map(
        body,
        mesh=mesh,
        in_specs=placed,
        out_specs=(
            P("dp", None, "tensor"),
            P("dp", None, "tensor"),
            P("dp", None, "tensor"),
            P("tensor", None),
            P("tensor"),
            P(),
        ),
        check_vma=False,
    )
```
